512 devices in a mesh: section: 16 (over y, core), tensor: 8 (over z), dp: 4 (over x).
Axes of the slice: x: 4, y: 8, z: 8, core: 2. Of those that a mesh axis runs over, the one named last changes fastest.
Arguments:
- section_out: bfloat16 [16, 512, 12288], P('section', 'dp', 'tensor'), may hold values from -6 to 6
- embedded: bfloat16 [512, 12288], P('dp', 'tensor'), may hold values from -6 to 6
- section_grad: bfloat16 [16, 512, 12288], P('section', 'dp', 'tensor'), may hold values from -0.26367188 to 0.26367188
- loss_grad: bfloat16 [512, 12288], P('dp', 'tensor'), may hold values from -0.26367188 to 0.26367188
- assign: int32 [16, 96, 1], P('section', 'tensor'), may hold values from 0 to 15; in each aligned block of 12 rows (0 to 11, 12 to 23, ..., all dimensions but the last counted through in order) at most 2 rows name the same one
- state_a: bfloat16 [16, 256, 128, 128], P('section', 'tensor'), may hold values from -6 to 54, as said below
- state_g: bfloat16 [16, 256, 128, 128], P('section', 'tensor'), may hold values from -6 to 54, as said below
Outputs:
- update: float32 [16, 96, 128, 128], P('section', 'tensor')
The draws below stay inside these ranges and needn't reach their ends.
Inputs may be any that keep to these rules, and one draw needn't show every extreme that they name: `assign`: within the rows of one device (aligned blocks of 12 rows along the first two dimensions), no section is named more than 2 times, a bound that some block reaches. `state_a`: each block is symmetric. `state_g`: each block is symmetric.
All inputs are finite; a program needn't handle non-finite values. Where the reference program divides by a largest or mean magnitude, that divisor is 1e-20 or more.
Results may differ from the reference program's by a relative error of at most 0.0003.
Values may be sent and summed in bfloat16 or wider, within the bound.
No kernel may reach another device: no remote copies, remote signals or barrier semaphores. Data moves between devices by JAX's collectives and lax.ppermute only.
A program may use at most 64 MiB of HBM per device.

```python
import math
import jax
import jax.numpy as jnp
import numpy as np
from jax import lax

D = 12288
BLK = 128
NS_ITERS = 5
SECTIONS = 16
TOKENS = 512
NBLK = 96
NB_DEV = 12
CAP = 2
SLOTS = 32
HOLD = 256
N_SECTION = 16
N_TENSOR = 8


def factor_blocks(key, spread):
    shape_full = (SECTIONS, HOLD, BLK, BLK)
    noise_key, diagonal_key = jax.random.split(key)
    noise_part = jax.random.normal(noise_key, shape_full, jnp.float32) * spread
    symmetric = (noise_part + jnp.swapaxes(noise_part, -1, -2)) * 0.7071
    diagonal = jax.random.uniform(diagonal_key, (SECTIONS, HOLD, BLK), jnp.float32, 1.0, 3.0)
    identity = jnp.eye(BLK, dtype=jnp.float32)
    return symmetric + identity * diagonal[..., None]


def draw_state_a(key, part):
    key = jax.random.fold_in(key, 7)
    blocks = factor_blocks(key, 0.03)
    return blocks.astype(jnp.bfloat16)


def draw_state_g(key, part):
    key = jax.random.fold_in(key, 13)
    blocks = factor_blocks(key, 0.03)
    return blocks.astype(jnp.bfloat16)


def block_scale(stream_key, shape, cuts, smallest, top_value):
    gain = 1.0
    for axis_at, parts in cuts:
        draws = jax.random.uniform(jax.random.fold_in(jax.random.fold_in(stream_key, 6), axis_at), (parts,), jnp.float32, smallest / len(cuts), top_value / len(cuts))
        gain = gain * jnp.repeat(jnp.exp(draws), shape[axis_at] // parts).reshape((-1,) + (1,) * (len(shape) - 1 - axis_at))
    return gain


def assign_block(key, own, number, rows, amount, top, most, lean):
    ranking = jax.random.permutation(key, amount)
    heavy_load, usual = load_shares(amount, rows * top, most, lean, True), load_shares(amount, rows * top, most, lean, False)
    places = jnp.arange(amount)

    def named(tallies, rotation):
        used = int((tallies > 0).sum())
        fixed = max(1, used // 4)
        shifted = fixed + (places - fixed + rotation * (used - fixed)) % max(1, amount - fixed)
        return jnp.zeros((amount,), jnp.int32).at[ranking[jnp.where(places < fixed, places, shifted)]].set(jnp.asarray(tallies, jnp.int32))

    tallies = jnp.where(number % 4 == 0, named(heavy_load, number // 4), named(usual, number - number // 4 - 1))
    mixed = jax.random.permutation(jax.random.fold_in(own, 3), amount)
    donor, sink = mixed[0:amount // 2 * 2:2], mixed[1:amount // 2 * 2:2]
    margin = jnp.minimum(tallies[donor] - 1, most - tallies[sink]) // 2
    margin = jnp.where((donor == ranking[0]) | (sink == ranking[0]) | (tallies[sink] == 0), 0, jnp.maximum(margin, 0))
    shifted = jax.random.randint(jax.random.fold_in(own, 4), (amount // 2,), 0, 1 << 20) % (margin + 1)
    tallies = tallies.at[donor].add(-shifted).at[sink].add(shifted)
    items = jnp.searchsorted(jnp.cumsum(tallies), jnp.arange(rows * top), side="right").astype(jnp.int32)
    listing = items.reshape(top, rows).T
    listing = listing[jax.random.permutation(jax.random.fold_in(own, 1), rows)]
    rotation = jax.random.randint(jax.random.fold_in(own, 2), (rows, 1), 0, top)
    return jnp.take_along_axis(listing, (jnp.arange(top)[None, :] + rotation) % top, axis=1)


def load_shares(amount, total, bound, skew, full):
    weights = [(1 << 20) // math.isqrt(grade ** skew) + 1 for grade in range(1, amount + 1)]
    largest = bound if full else min(bound, max(-(-total // amount), total * weights[0] // sum(weights)))
    least = 1 if total - largest >= amount - 1 else 0
    counts, surplus = [largest] + [least] * (amount - 1), total - largest - least * (amount - 1)
    while surplus > 0:
        movable = [i for i in range(1, amount) if counts[i] < largest] or [i for i in range(1, amount) if counts[i] < bound]
        pool, remaining = sum([weights[i] for i in movable]), surplus
        for i in movable:
            addition = min(bound - counts[i], max(1, remaining * weights[i] // pool), surplus)
            counts[i] = counts[i] + addition
            surplus = surplus - addition
    return np.array(counts)


def bell_draw(own_key, shape, width, limit, cuts=(), held_as=jnp.bfloat16):
    loudness = block_scale(own_key, shape, cuts, -0.22, 0.18) if cuts else 1.0
    array = jax.random.normal(own_key, shape, jnp.float32) * width * loudness
    return jnp.minimum(jnp.maximum(array, -limit), limit).astype(held_as)


def setup_inputs(seed: int = 0) -> dict:
    keys = jax.random.split(jax.random.key(seed), 8)
    section_out = bell_draw(keys[0], (SECTIONS, TOKENS, D), 1.0, 6.0, ((0, 16), (1, 4), (2, 8)))
    embedded = bell_draw(keys[1], (TOKENS, D), 1.0, 6.0, ((0, 4), (1, 8)))
    section_grad = bell_draw(keys[2], (SECTIONS, TOKENS, D), (TOKENS ** -0.5), 0.26367188, ((0, 16), (1, 4), (2, 8)))
    loss_grad = bell_draw(keys[3], (TOKENS, D), (TOKENS ** -0.5), 0.26367188, ((0, 4), (1, 8)))
    assign_keys = jax.random.split(jax.random.fold_in(keys[4], 1), SECTIONS * NBLK // NB_DEV)
    assign_turns = jax.random.permutation(jax.random.fold_in(keys[4], 3), SECTIONS * NBLK // NB_DEV)
    assign = jax.vmap(lambda own, number: assign_block(jax.random.fold_in(keys[4], 2), own, number, NB_DEV, N_SECTION, 1, CAP, 2))(assign_keys, assign_turns).reshape((SECTIONS, NBLK, 1))
    state_a = draw_state_a(jax.random.fold_in(keys[7], 71), 0)
    state_g = draw_state_g(jax.random.fold_in(keys[7], 71), 0)
    return dict(section_out=section_out, embedded=embedded, section_grad=section_grad, loss_grad=loss_grad, assign=assign, state_a=state_a, state_g=state_g)


HIGH = lax.Precision.HIGHEST


def newton_inverse(matrix):
    extent = matrix.shape[-1]
    identity = jnp.eye(extent, dtype=matrix.dtype)
    row_bound = jnp.max(jnp.sum(jnp.abs(matrix), axis=-1), axis=-1)
    approx = identity / row_bound[..., None, None]
    for repeat in range(NS_ITERS):
        product = jnp.matmul(matrix, approx, precision=HIGH)
        approx = jnp.matmul(approx, 2.0 * identity - product, precision=HIGH)
    return approx


def precondition(held_a, held_g, batch_a, batch_g, gradient):
    identity = jnp.eye(batch_a.shape[-1], dtype=jnp.float32)
    matrix_a = 0.5 * held_a.astype(jnp.float32) + 0.5 * batch_a + 0.1 * identity
    matrix_g = 0.5 * held_g.astype(jnp.float32) + 0.5 * batch_g + 0.1 * identity
    inv_a = newton_inverse(matrix_a)
    inv_g = newton_inverse(matrix_g)
    return jnp.matmul(jnp.matmul(inv_a, gradient, precision=HIGH), inv_g, precision=HIGH)


def section_stats(section_pair):
    inputs, out_grad = section_pair
    in_blocks = inputs.astype(jnp.float32).reshape(TOKENS, NBLK, BLK)
    grad_blocks = out_grad.astype(jnp.float32).reshape(TOKENS, NBLK, BLK)
    gram_in = jnp.einsum('tnb,tnc->nbc', in_blocks, in_blocks, precision=HIGH) / TOKENS
    gram_out = jnp.einsum('tnb,tnc->nbc', grad_blocks, grad_blocks, precision=HIGH)
    cross = jnp.einsum('tnb,tnc->nbc', in_blocks, grad_blocks, precision=HIGH)
    return gram_in, gram_out, cross


def reference(section_out, embedded, section_grad, loss_grad, assign, state_a, state_g):
    inputs = jnp.concatenate([embedded[None], section_out[:-1]], axis=0)
    out_grad = jnp.concatenate([section_grad[1:], loss_grad[None]], axis=0)
    batch_a, batch_g, gradient = lax.map(section_stats, (inputs, out_grad))
    holder = assign[:, :, 0].astype(jnp.int32)
    target = holder.reshape(SECTIONS, N_TENSOR, NB_DEV)
    block_order = jnp.arange(NB_DEV, dtype=jnp.int32)
    earlier = block_order[None, :] < block_order[:, None]
    same_dest = (target[..., :, None] == target[..., None, :]) & earlier
    rank_in = jnp.sum(same_dest.astype(jnp.int32), axis=-1)
    tensor_pos = jnp.arange(N_TENSOR, dtype=jnp.int32)[None, :, None]
    section_pos = jnp.arange(SECTIONS, dtype=jnp.int32)[:, None, None]
    slot_index = (tensor_pos * SLOTS + section_pos * CAP + rank_in).reshape(SECTIONS, NBLK).astype(jnp.int32)
    held_a = state_a[holder, slot_index]
    held_g = state_g[holder, slot_index]
    return precondition(held_a, held_g, batch_a, batch_g, gradient)
```

```python
import functools

import jax
import jax.numpy as jnp
from jax import lax
from jax.experimental import pallas as pl
from jax.experimental.pallas import tpu as pltpu
from jax.sharding import PartitionSpec as P

BLK = 128
NS_ITERS = 5
DAMPING = 0.1
DP = 4


def pack_state_kernel(part_ref, a_ref, g_ref, out_ref):
    out_ref[:, 0] = a_ref[...]
    out_ref[:, 1] = g_ref[...]


def pack_state(state_a, state_g, part):
    slots = state_a.shape[0]
    rows = BLK // DP
    block = pl.BlockSpec((slots, rows, BLK), lambda i, part: (0, part[0], 0))
    return pl.pallas_call(
        pack_state_kernel,
        out_shape=jax.ShapeDtypeStruct((slots, 2, rows, BLK), state_a.dtype),
        grid_spec=pltpu.PrefetchScalarGridSpec(
            num_scalar_prefetch=1,
            grid=(1,),
            in_specs=[block, block],
            out_specs=pl.BlockSpec((slots, 2, rows, BLK), lambda i, part: (0, 0, 0, 0)),
        ),
        name="pack_state",
    )(part, state_a, state_g)


def pack_tokens_kernel(section_ref, out_ref, embedded_ref, grad_ref, loss_ref, in_send, grad_send):
    width = in_send.shape[2]
    section = section_ref[0]
    last = section_ref[1]

    @pl.when(section == last)
    def _():
        for part in range(DP):
            in_send[part] = embedded_ref[:, part * width:(part + 1) * width]

    @pl.when(section != last)
    def _():
        for part in range(DP):
            in_send[part] = out_ref[:, part * width:(part + 1) * width]

    @pl.when(section == 0)
    def _():
        for part in range(DP):
            grad_send[part] = loss_ref[:, part * width:(part + 1) * width]

    @pl.when(section != 0)
    def _():
        for part in range(DP):
            grad_send[part] = grad_ref[:, part * width:(part + 1) * width]


def pack_tokens(place, section_out, embedded, section_grad, loss_grad):
    tokens, features = section_out.shape
    shape = jax.ShapeDtypeStruct((DP, tokens, features // DP), section_out.dtype)
    vmem = pl.BlockSpec(memory_space=pltpu.VMEM)
    return pl.pallas_call(
        pack_tokens_kernel,
        out_shape=(shape, shape),
        in_specs=[pl.BlockSpec(memory_space=pltpu.SMEM)] + [vmem] * 4,
        out_specs=(vmem, vmem),
        name="pack_tokens",
    )(place, section_out, embedded, section_grad, loss_grad)


def select_kernel(assign_ref, got_ref, out_ref):
    count = out_ref.shape[0]
    holders = [assign_ref[j] for j in range(count)]
    for j in range(count):
        rank = jnp.int32(0)
        for earlier in range(j):
            rank = rank + (holders[earlier] == holders[j]).astype(jnp.int32)
        out_ref[j] = got_ref[holders[j] * 2 + rank]


def select(assign, got):
    vmem = pl.BlockSpec(memory_space=pltpu.VMEM)
    return pl.pallas_call(
        select_kernel,
        out_shape=jax.ShapeDtypeStruct((assign.shape[0],) + got.shape[1:], got.dtype),
        in_specs=[pl.BlockSpec(memory_space=pltpu.SMEM), vmem],
        out_specs=vmem,
        name="select",
    )(assign, got)


def halves(value):
    high = value.astype(jnp.bfloat16)
    low = (value - high.astype(jnp.float32)).astype(jnp.bfloat16)
    return high, low


def product(left, right):
    lhs = jnp.concatenate([left[0], left[0], left[1]], axis=1)
    rhs = jnp.concatenate([right[0], right[1], right[0]], axis=0)
    return jnp.dot(lhs, rhs, preferred_element_type=jnp.float32)


def precondition_kernel(tokens_total, x_ref, held_ref, out_ref):
    count = out_ref.shape[0]
    chunks, _, tokens, _ = x_ref.shape
    row = lax.broadcasted_iota(jnp.int32, (BLK, BLK), 0)
    column = lax.broadcasted_iota(jnp.int32, (BLK, BLK), 1)
    identity = (row == column).astype(jnp.float32)

    def start(matrix):
        bound = jnp.max(jnp.sum(jnp.abs(matrix), axis=0, keepdims=True), axis=1, keepdims=True)
        return identity - matrix / bound, bound

    rest_a, rest_g, value, bound_g = [], [], [], []
    for j in range(count):
        columns = slice(j * BLK, (j + 1) * BLK)
        both = jnp.concatenate(
            [
                x_ref[:, 0, :, columns].reshape(chunks * tokens, BLK),
                x_ref[:, 1, :, columns].reshape(chunks * tokens, BLK),
            ],
            axis=1,
        )
        sums = lax.dot_general(both, both, (((0,), (0,)), ((), ())), preferred_element_type=jnp.float32)
        held_a = held_ref[:, j, 0].reshape(BLK, BLK).astype(jnp.float32)
        held_g = held_ref[:, j, 1].reshape(BLK, BLK).astype(jnp.float32)
        batch_a = sums[:BLK, :BLK] / tokens_total
        matrix_a = 0.5 * held_a + 0.5 * batch_a + DAMPING * identity
        matrix_g = 0.5 * held_g + 0.5 * sums[BLK:, BLK:] + DAMPING * identity
        left, bound_a = start(matrix_a)
        right, bound = start(matrix_g)
        rest_a.append(left)
        rest_g.append(right)
        value.append(sums[:BLK, BLK:] / bound_a)
        bound_g.append(bound)
    for step in range(NS_ITERS):
        for j in range(count):
            left, right, middle = halves(rest_a[j]), halves(rest_g[j]), halves(value[j])
            if step < NS_ITERS - 1:
                rhs = [jnp.concatenate([l, m], axis=1) for l, m in zip(left, middle)]
                both = product(left, rhs)
                rest_a[j] = both[:, :BLK]
                value[j] = value[j] + both[:, BLK:]
                middle = halves(value[j])
                lhs = [jnp.concatenate([r, m], axis=0) for r, m in zip(right, middle)]
                both = product(lhs, right)
                rest_g[j] = both[:BLK]
                value[j] = value[j] + both[BLK:]
            else:
                value[j] = value[j] + product(left, middle)
                value[j] = value[j] + product(halves(value[j]), right)
    for j in range(count):
        out_ref[j] = value[j] / bound_g[j]


def precondition(x, held, tokens_total):
    count = held.shape[1]
    vmem = pl.BlockSpec(memory_space=pltpu.VMEM)
    return pl.pallas_call(
        functools.partial(precondition_kernel, tokens_total),
        out_shape=jax.ShapeDtypeStruct((count, BLK, BLK), jnp.float32),
        in_specs=[vmem, vmem],
        out_specs=vmem,
        compiler_params=pltpu.CompilerParams(vmem_limit_bytes=32 * 1024 * 1024),
        name="precondition",
    )(x, held)


def spread(array, axis):
    return lax.all_to_all(array, axis, split_axis=0, concat_axis=0, tiled=True)


def body(section_out, embedded, section_grad, loss_grad, assign, state_a, state_g):
    section = lax.axis_index("section")
    sections = lax.axis_size("section")
    part = lax.axis_index("dp")
    slots = state_a.shape[1]
    blocks = assign.shape[1]
    tokens, features = embedded.shape
    rows = BLK // DP

    packed = pack_state(state_a[0], state_g[0], part.astype(jnp.int32).reshape(1))
    got = spread(packed.reshape(sections, slots // sections * 2 * rows, BLK), "section")

    place = jnp.stack([section, jnp.full_like(section, sections - 1)]).astype(jnp.int32)
    in_send, grad_send = pack_tokens(place, section_out[0], embedded, section_grad[0], loss_grad)
    inputs = lax.ppermute(in_send, "section", [(i, (i + 1) % sections) for i in range(sections)])
    grads = lax.ppermute(grad_send, "section", [(i, (i - 1) % sections) for i in range(sections)])
    x = spread(jnp.stack([inputs, grads], axis=1), "dp")

    mine = select(assign[0, :, 0], got.reshape(slots, 2 * rows, BLK))
    held = spread(mine.reshape(DP, blocks // DP * 2 * rows, BLK), "dp")
    result = precondition(x, held.reshape(DP, blocks // DP, 2, rows, BLK), tokens * DP)
    return lax.all_gather(result, "dp", axis=0, tiled=True)[None]


def solution(mesh):
    in_specs = (
        P("section", "dp", "tensor"),
        P("dp", "tensor"),
        P("section", "dp", "tensor"),
        P("dp", "tensor"),
        P("section", "tensor", None),
        P("section", "tensor", None, None),
        P("section", "tensor", None, None),
    )
    out_specs = P("section", "tensor", None, None)
    return jax.shard_map(body, mesh=mesh, in_specs=in_specs, out_specs=out_specs, check_vma=False)
```

```python
import functools

import jax
import jax.numpy as jnp
from jax import lax
from jax.experimental import pallas as pl
from jax.experimental.pallas import tpu as pltpu
from jax.sharding import PartitionSpec as P

BLK = 128
NS_ITERS = 5
DAMPING = 0.1
DP = 4
PIECES = 4


SMALL = pltpu.CompilerParams(vmem_limit_bytes=4 * 1024 * 1024)
ANY = pl.BlockSpec(memory_space=pl.ANY)
VMEM = pl.BlockSpec(memory_space=pltpu.VMEM)
SMEM = pl.BlockSpec(memory_space=pltpu.SMEM)


def run(copies, sems):
    made = [pltpu.make_async_copy(source, target, sems.at[i]) for i, (source, target) in enumerate(copies)]
    for copy in made:
        copy.start()
    for copy in made:
        copy.wait()


def pack_state_kernel(a_ref, g_ref, out_ref, sems):
    slots, _, rows, _ = out_ref.shape
    mine = pl.ds(pl.multiple_of(lax.axis_index("dp") * rows, rows), rows)
    copies = []
    for first in range(0, slots, slots // PIECES):
        piece = pl.ds(first, slots // PIECES)
        copies.append((a_ref.at[piece, mine, :], out_ref.at[piece, 0]))
        copies.append((g_ref.at[piece, mine, :], out_ref.at[piece, 1]))
    run(copies, sems)


def pack_state(state_a, state_g):
    state_a = pltpu.with_memory_space_constraint(state_a, pltpu.HBM)
    state_g = pltpu.with_memory_space_constraint(state_g, pltpu.HBM)
    return pl.pallas_call(
        pack_state_kernel,
        out_shape=pltpu.VMEM((state_a.shape[0], 2, BLK // DP, BLK), state_a.dtype),
        in_specs=[ANY, ANY],
        out_specs=VMEM,
        scratch_shapes=[pltpu.SemaphoreType.DMA((2 * PIECES,))],
        compiler_params=SMALL,
        name="pack_state",
    )(state_a, state_g)


def pack_tokens_kernel(assign_ref, arrived_ref, embedded_ref, returned_ref, loss_ref, *refs):
    send_refs, slot_ref, sems = refs[:-2], refs[-2], refs[-1]
    for j in range(assign_ref.shape[0]):
        rank = jnp.int32(0)
        for earlier in range(j):
            rank = rank + (assign_ref[earlier] == assign_ref[j]).astype(jnp.int32)
        slot_ref[j] = assign_ref[j] * 2 + rank
    width = send_refs[0].shape[2]
    section, part = lax.axis_index("section"), lax.axis_index("dp")
    last_section = lax.axis_size("section") - 1

    for first in (True, False):
        for last in (True, False):
            if first and last:
                continue

            @pl.when(((section == 0) == first) & ((section == last_section) == last))
            def _():
                copies = []
                for which, source in enumerate((embedded_ref if first else arrived_ref, loss_ref if last else returned_ref)):
                    for turn in range(DP):
                        start = pl.multiple_of(lax.rem(part + turn, DP) * width, width)
                        copies.append((source.at[:, pl.ds(start, width)], send_refs[turn].at[which]))
                run(copies, sems)


def pack_tokens(assign, arrived, embedded, returned, loss_grad):
    tokens, features = arrived.shape
    shape = jax.ShapeDtypeStruct((2, tokens, features // DP), arrived.dtype)
    return pl.pallas_call(
        pack_tokens_kernel,
        out_shape=(shape,) * DP + (pltpu.SMEM(assign.shape, jnp.int32),),
        in_specs=[SMEM] + [ANY] * 4,
        out_specs=(ANY,) * DP + (SMEM,),
        scratch_shapes=[pltpu.SemaphoreType.DMA((2 * DP,))],
        compiler_params=SMALL,
        cost_estimate=pl.CostEstimate(flops=15 * 10**9, bytes_accessed=2**20, transcendentals=0),
        name="pack_tokens",
    )(assign, arrived, embedded, returned, loss_grad)


def select_kernel(slot_ref, got_ref, out_ref):
    for j in range(out_ref.shape[0]):
        out_ref[j] = got_ref[slot_ref[j]]


def select(slot, got):
    return pl.pallas_call(
        select_kernel,
        out_shape=jax.ShapeDtypeStruct((slot.shape[0],) + got.shape[1:], got.dtype),
        in_specs=[SMEM, VMEM],
        out_specs=VMEM,
        compiler_params=SMALL,
        name="select",
    )(slot, got)


def halves(value):
    high = value.astype(jnp.bfloat16)
    low = (value - high.astype(jnp.float32)).astype(jnp.bfloat16)
    return high, low


def product(left, right):
    lhs = jnp.concatenate([left[0], left[0], left[1]], axis=1)
    rhs = jnp.concatenate([right[0], right[1], right[0]], axis=0)
    return jnp.dot(lhs, rhs, preferred_element_type=jnp.float32)


def gram_kernel(*refs):
    chunk_refs, out_ref = refs[:-1], refs[-1]
    for j in range(out_ref.shape[0]):
        columns = slice(j * BLK, (j + 1) * BLK)
        inputs = jnp.concatenate([ref[0, :, columns] for ref in chunk_refs], axis=0)
        grads = jnp.concatenate([ref[1, :, columns] for ref in chunk_refs], axis=0)
        both = jnp.concatenate([inputs, grads], axis=1)
        out_ref[j] = lax.dot_general(both, both, (((0,), (0,)), ((), ())), preferred_element_type=jnp.float32)


def gram(chunks):
    return pl.pallas_call(
        gram_kernel,
        out_shape=jax.ShapeDtypeStruct((chunks[0].shape[2] // BLK, 2 * BLK, 2 * BLK), jnp.float32),
        in_specs=[VMEM] * DP,
        out_specs=VMEM,
        compiler_params=pltpu.CompilerParams(vmem_limit_bytes=8 * 1024 * 1024),
        cost_estimate=pl.CostEstimate(flops=10**9, bytes_accessed=2**20, transcendentals=0),
        name="gram",
    )(*chunks)


def precondition_kernel(tokens_total, sums_ref, held_ref, out_ref):
    count = out_ref.shape[0]
    row = lax.broadcasted_iota(jnp.int32, (BLK, BLK), 0)
    column = lax.broadcasted_iota(jnp.int32, (BLK, BLK), 1)
    identity = (row == column).astype(jnp.float32)

    def start(matrix):
        bound = jnp.max(jnp.sum(jnp.abs(matrix), axis=0, keepdims=True), axis=1, keepdims=True)
        return identity - matrix / bound, bound

    rest_a, rest_g, value, bound_g = [], [], [], []
    for j in range(count):
        held_a = held_ref[:, j, 0].reshape(BLK, BLK).astype(jnp.float32)
        held_g = held_ref[:, j, 1].reshape(BLK, BLK).astype(jnp.float32)
        batch_a = sums_ref[j, :BLK, :BLK] / tokens_total
        batch_g = sums_ref[j, BLK:, BLK:]
        left, bound_a = start(0.5 * held_a + 0.5 * batch_a + DAMPING * identity)
        right, bound = start(0.5 * held_g + 0.5 * batch_g + DAMPING * identity)
        rest_a.append(left)
        rest_g.append(right)
        value.append(sums_ref[j, :BLK, BLK:] / bound_a)
        bound_g.append(bound)
    for step in range(NS_ITERS):
        for j in range(count):
            left, right, middle = halves(rest_a[j]), halves(rest_g[j]), halves(value[j])
            if step < NS_ITERS - 1:
                rhs = [jnp.concatenate([l, m], axis=1) for l, m in zip(left, middle)]
                both = product(left, rhs)
                rest_a[j] = both[:, :BLK]
                value[j] = value[j] + both[:, BLK:]
                middle = halves(value[j])
                lhs = [jnp.concatenate([r, m], axis=0) for r, m in zip(right, middle)]
                both = product(lhs, right)
                rest_g[j] = both[:BLK]
                value[j] = value[j] + both[BLK:]
            else:
                value[j] = value[j] + product(left, middle)
                value[j] = value[j] + product(halves(value[j]), right)
    for j in range(count):
        out_ref[j] = value[j] / bound_g[j]


def precondition(sums, held, tokens_total):
    return pl.pallas_call(
        functools.partial(precondition_kernel, tokens_total),
        out_shape=jax.ShapeDtypeStruct((held.shape[1], BLK, BLK), jnp.float32),
        in_specs=[VMEM, VMEM],
        out_specs=VMEM,
        compiler_params=pltpu.CompilerParams(vmem_limit_bytes=8 * 1024 * 1024),
        name="precondition",
    )(sums, held)


def spread(array, axis):
    return lax.all_to_all(array, axis, split_axis=0, concat_axis=0, tiled=True)


def hop(array, axis, by):
    size = lax.axis_size(axis)
    return lax.ppermute(array, axis, [(i, (i + by) % size) for i in range(size)])


def body(section_out, embedded, section_grad, loss_grad, assign, state_a, state_g):
    sections = lax.axis_size("section")
    slots = state_a.shape[1]
    blocks = assign.shape[1]
    tokens, features = embedded.shape
    rows = BLK // DP

    arrived = hop(section_out[0], "section", 1)
    packed, section_grad = lax.optimization_barrier((pack_state(state_a[0], state_g[0]), section_grad))
    returned = hop(section_grad[0], "section", -1)
    got = spread(packed.reshape(sections, slots // sections * 2 * rows, BLK), "section")

    *sends, slot = pack_tokens(assign[0, :, 0], arrived, embedded, returned, loss_grad)
    chunks = [sends[0]] + [hop(sends[turn], "dp", turn) for turn in range(1, DP)]

    mine = select(slot, got.reshape(slots, 2 * rows, BLK))
    held = spread(mine.reshape(DP, blocks // DP * 2 * rows, BLK), "dp")
    held = held.reshape(DP, blocks // DP, 2, rows, BLK)

    result = precondition(gram(chunks), held, tokens * DP)
    return lax.all_gather(result, "dp", axis=0, tiled=True)[None]


def solution(mesh):
    in_specs = (
        P("section", "dp", "tensor"),
        P("dp", "tensor"),
        P("section", "dp", "tensor"),
        P("dp", "tensor"),
        P("section", "tensor", None),
        P("section", "tensor", None, None),
        P("section", "tensor", None, None),
    )
    out_specs = P("section", "tensor", None, None)
    return jax.shard_map(body, mesh=mesh, in_specs=in_specs, out_specs=out_specs, check_vma=False)
```

```python
import functools

import jax
import jax.numpy as jnp
from jax import lax
from jax.experimental import pallas as pl
from jax.experimental.pallas import tpu as pltpu
from jax.sharding import PartitionSpec as P

BLK = 128
NS_ITERS = 5
DAMPING = 0.1
DP = 4
TILE = BLK // DP
CORNER = TILE // 2


SMALL = pltpu.CompilerParams(vmem_limit_bytes=4 * 1024 * 1024)
ANY = pl.BlockSpec(memory_space=pl.ANY)
VMEM = pl.BlockSpec(memory_space=pltpu.VMEM)
SMEM = pl.BlockSpec(memory_space=pltpu.SMEM)


def run(copies, sems):
    made = [pltpu.make_async_copy(source, target, sems.at[i]) for i, (source, target) in enumerate(copies)]
    for copy in made:
        copy.start()
    for copy in made:
        copy.wait()


def lane_tile(shape):
    return lax.broadcasted_iota(jnp.int32, shape, len(shape) - 1) // TILE


def turned(value, tiles):
    if isinstance(tiles, int):
        shift = tiles * TILE % BLK
        return pltpu.roll(value, shift, value.ndim - 1) if shift else value
    return pltpu.roll(value, lax.rem(tiles * TILE + 2 * BLK, BLK), value.ndim - 1)


def pack_state_kernel(a_ref, g_ref, out_ref, strip, corner, sems):
    part = lax.axis_index("dp")
    odd = lax.rem(part, 2)
    rows = pl.ds(pl.multiple_of(part * TILE, TILE), TILE)
    half = pl.ds(pl.multiple_of(odd * TILE + lax.div(part, 2) * CORNER, CORNER), CORNER)
    copies = []
    for which, ref in enumerate((a_ref, g_ref)):
        copies.append((ref.at[:, rows, :], strip.at[which]))
        copies.append((ref.at[:, half, :], corner.at[which]))
    run(copies, sems)

    sections = out_ref.shape[0]
    a, g = (strip[which].astype(jnp.float32).reshape(-1, BLK) for which in range(2))
    pairs = jnp.where(lane_tile(a.shape) < 2, turned(a, -part), turned(g, 2 - part))
    out_ref[:, :2 * TILE] = pairs.astype(out_ref.dtype).reshape(sections, 2 * TILE, BLK)

    a, g = (corner[which].astype(jnp.float32).reshape(sections, 2, CORNER, BLK) for which in range(2))
    tile = lane_tile((sections * CORNER, BLK))
    last = jnp.zeros(tile.shape, jnp.float32)
    for place, source in enumerate((a[:, 0], g[:, 0], a[:, 1], g[:, 1])):
        last = jnp.where(tile == place, turned(source.reshape(tile.shape), place - 2 - odd), last)
    out_ref[:, 2 * TILE:] = last.astype(out_ref.dtype).reshape(sections, CORNER, BLK)


def pack_state(state_a, state_g):
    slots = state_a.shape[0]
    state_a = pltpu.with_memory_space_constraint(state_a, pltpu.HBM)
    state_g = pltpu.with_memory_space_constraint(state_g, pltpu.HBM)
    return pl.pallas_call(
        pack_state_kernel,
        out_shape=pltpu.VMEM((slots // 2, 2 * TILE + CORNER, BLK), state_a.dtype),
        in_specs=[ANY, ANY],
        out_specs=VMEM,
        scratch_shapes=[
            pltpu.VMEM((2, slots, TILE, BLK), state_a.dtype),
            pltpu.VMEM((2, slots, CORNER, BLK), state_a.dtype),
            pltpu.SemaphoreType.DMA((4,)),
        ],
        compiler_params=pltpu.CompilerParams(vmem_limit_bytes=6 * 1024 * 1024),
        name="pack_state",
    )(state_a, state_g)


def pack_tokens_kernel(assign_ref, arrived_ref, embedded_ref, returned_ref, loss_ref, *refs):
    send_refs, (slot_ref, holder_ref, sems, holder_sem) = refs[:DP], refs[DP:]
    holders = pltpu.make_async_copy(assign_ref, holder_ref, holder_sem)
    holders.start()
    width = send_refs[0].shape[2]
    section, part = lax.axis_index("section"), lax.axis_index("dp")
    last_section = lax.axis_size("section") - 1

    for first in (True, False):
        for last in (True, False):
            if first and last:
                continue

            @pl.when(((section == 0) == first) & ((section == last_section) == last))
            def _():
                copies = []
                for which, source in enumerate((embedded_ref if first else arrived_ref, loss_ref if last else returned_ref)):
                    for turn in range(DP):
                        start = pl.multiple_of(lax.rem(part + turn, DP) * width, width)
                        copies.append((source.at[:, pl.ds(start, width)], send_refs[turn].at[which]))
                run(copies, sems)

    holders.wait()
    for j in range(holder_ref.shape[0]):
        rank = jnp.int32(0)
        for earlier in range(j):
            rank = rank + (holder_ref[earlier] == holder_ref[j]).astype(jnp.int32)
        slot_ref[j] = holder_ref[j] * 2 + rank


def pack_tokens(assign, arrived, embedded, returned, loss_grad):
    tokens, features = arrived.shape
    shape = jax.ShapeDtypeStruct((2, tokens, features // DP), arrived.dtype)
    assign = pltpu.with_memory_space_constraint(assign, pltpu.HBM)
    return pl.pallas_call(
        pack_tokens_kernel,
        out_shape=(shape,) * DP + (pltpu.SMEM(assign.shape, jnp.int32),),
        in_specs=[ANY] * 5,
        out_specs=(ANY,) * DP + (SMEM,),
        scratch_shapes=[
            pltpu.SMEM(assign.shape, jnp.int32),
            pltpu.SemaphoreType.DMA((2 * DP,)),
            pltpu.SemaphoreType.DMA,
        ],
        compiler_params=SMALL,
        cost_estimate=pl.CostEstimate(flops=15 * 10**9, bytes_accessed=2**20, transcendentals=0),
        name="pack_tokens",
    )(assign, arrived, embedded, returned, loss_grad)


def select_kernel(slot_ref, got_ref, out_ref):
    blocks = slot_ref.shape[0] // DP
    low = lane_tile((CORNER, BLK)) < 2
    for part in range(DP):
        corners = []
        for j in range(blocks):
            slot = slot_ref[part * blocks + j]
            holder, rank = lax.div(slot, 2), lax.rem(slot, 2)
            mine = pl.ds(pl.multiple_of(rank * TILE, TILE), TILE)
            out_ref[part, j * TILE:(j + 1) * TILE] = got_ref[holder, mine, :]
            corner = got_ref[holder, 2 * TILE:, :].astype(jnp.float32)
            corners.append(turned(corner, 2 * lax.rem(rank + j, 2)))
        for j in range(0, blocks, 2):
            both = jnp.where(low, corners[j], corners[min(j + 1, blocks - 1)])
            start = blocks * TILE + j // 2 * CORNER
            out_ref[part, start:start + CORNER] = both.astype(out_ref.dtype)


def select(slot, got):
    blocks = slot.shape[0] // DP
    return pl.pallas_call(
        select_kernel,
        out_shape=jax.ShapeDtypeStruct((DP, blocks * TILE + (blocks + 1) // 2 * CORNER, BLK), got.dtype),
        in_specs=[SMEM, VMEM],
        out_specs=VMEM,
        compiler_params=SMALL,
        name="select",
    )(slot, got)


def symmetric(held_ref, blocks, j, which):
    tile = lane_tile((TILE, BLK))
    start = blocks * TILE + j // 2 * CORNER
    corners = [held_ref[part, start:start + CORNER].astype(jnp.float32) for part in range(DP)]
    rows = []
    for part in range(DP):
        strip = turned(held_ref[part, j * TILE:(j + 1) * TILE].astype(jnp.float32), part - 2 * which)
        row = jnp.where(tile == part, 0.5 * strip, jnp.where(tile == (part + 1) % DP, strip, 0.0))
        if part < 2:
            corner = jnp.concatenate([corners[part], corners[part + 2]], axis=0)
            row = jnp.where(tile == part + 2, turned(corner, 2 + part - 2 * (j % 2) - which), row)
        rows.append(row)
    upper = jnp.concatenate(rows, axis=0)
    return upper + upper.T


def halves(value):
    high = value.astype(jnp.bfloat16)
    low = (value - high.astype(jnp.float32)).astype(jnp.bfloat16)
    return high, low


def product(left, right):
    lhs = jnp.concatenate([left[0], left[0], left[1]], axis=1)
    rhs = jnp.concatenate([right[0], right[1], right[0]], axis=0)
    return jnp.dot(lhs, rhs, preferred_element_type=jnp.float32)


def gram_kernel(*refs):
    chunk_refs, out_ref = refs[:-1], refs[-1]
    for j in range(out_ref.shape[0]):
        columns = slice(j * BLK, (j + 1) * BLK)
        inputs = jnp.concatenate([ref[0, :, columns] for ref in chunk_refs], axis=0)
        grads = jnp.concatenate([ref[1, :, columns] for ref in chunk_refs], axis=0)
        both = jnp.concatenate([inputs, grads], axis=1)
        out_ref[j] = lax.dot_general(both, both, (((0,), (0,)), ((), ())), preferred_element_type=jnp.float32)


def gram(chunks):
    return pl.pallas_call(
        gram_kernel,
        out_shape=jax.ShapeDtypeStruct((chunks[0].shape[2] // BLK, 2 * BLK, 2 * BLK), jnp.float32),
        in_specs=[VMEM] * DP,
        out_specs=VMEM,
        compiler_params=pltpu.CompilerParams(vmem_limit_bytes=8 * 1024 * 1024),
        cost_estimate=pl.CostEstimate(flops=10**9, bytes_accessed=2**20, transcendentals=0),
        name="gram",
    )(*chunks)


def precondition_kernel(tokens_total, sums_ref, held_ref, out_ref):
    count = out_ref.shape[0]
    row = lax.broadcasted_iota(jnp.int32, (BLK, BLK), 0)
    column = lax.broadcasted_iota(jnp.int32, (BLK, BLK), 1)
    identity = (row == column).astype(jnp.float32)
    blocks = [(j, which) for j in range(count) for which in range(2)]
    bound, rest, inverse = {}, {}, {}
    for j, which in blocks:
        held = symmetric(held_ref, count, j, which)
        batch = sums_ref[j, BLK:, BLK:] if which else sums_ref[j, :BLK, :BLK] / tokens_total
        matrix = 0.5 * held + 0.5 * batch + DAMPING * identity
        bound[j, which] = jnp.max(jnp.sum(jnp.abs(matrix), axis=0, keepdims=True), axis=1, keepdims=True)
        rest[j, which] = identity - matrix / bound[j, which]
    for block in blocks:
        inverse[block] = identity + rest[block]
        parts = halves(rest[block])
        rest[block] = product(parts, parts)
    for step in range(1, NS_ITERS):
        for block in blocks:
            left, right = halves(rest[block]), halves(inverse[block])
            if step < NS_ITERS - 1:
                both = product(left, [jnp.concatenate([l, r], axis=1) for l, r in zip(left, right)])
                rest[block] = both[:, :BLK]
                inverse[block] = inverse[block] + both[:, BLK:]
            else:
                inverse[block] = inverse[block] + product(left, right)
    half_done = [
        product(halves(inverse[j, 0]), halves(sums_ref[j, :BLK, BLK:] / bound[j, 0])) for j in range(count)
    ]
    for j in range(count):
        out_ref[j] = product(halves(half_done[j]), halves(inverse[j, 1])) / bound[j, 1]


def precondition(sums, held, tokens_total):
    return pl.pallas_call(
        functools.partial(precondition_kernel, tokens_total),
        out_shape=jax.ShapeDtypeStruct((sums.shape[0], BLK, BLK), jnp.float32),
        in_specs=[VMEM, VMEM],
        out_specs=VMEM,
        compiler_params=pltpu.CompilerParams(vmem_limit_bytes=8 * 1024 * 1024),
        name="precondition",
    )(sums, held)


def spread(array, axis):
    return lax.all_to_all(array, axis, split_axis=0, concat_axis=0, tiled=True)


def hop(array, axis, by):
    size = lax.axis_size(axis)
    return lax.ppermute(array, axis, [(i, (i + by) % size) for i in range(size)])


def body(section_out, embedded, section_grad, loss_grad, assign, state_a, state_g):
    tokens = embedded.shape[0]
    arrived = hop(section_out[0], "section", 1)
    packed, section_grad = lax.optimization_barrier((pack_state(state_a[0], state_g[0]), section_grad))
    returned = hop(section_grad[0], "section", -1)
    got = spread(packed, "section")

    *sends, slot = pack_tokens(assign[0, :, 0], arrived, embedded, returned, loss_grad)
    chunks = [sends[0]] + [hop(sends[turn], "dp", turn) for turn in range(1, DP)]

    held = spread(select(slot, got), "dp")

    result = precondition(gram(chunks), held, tokens * DP)
    return lax.all_gather(result, "dp", axis=0, tiled=True)[None]


def solution(mesh):
    in_specs = (
        P("section", "dp", "tensor"),
        P("dp", "tensor"),
        P("section", "dp", "tensor"),
        P("dp", "tensor"),
        P("section", "tensor", None),
        P("section", "tensor", None, None),
        P("section", "tensor", None, None),
    )
    out_specs = P("section", "tensor", None, None)
    return jax.shard_map(body, mesh=mesh, in_specs=in_specs, out_specs=out_specs, check_vma=False)
```

```python
import functools

import jax
import jax.numpy as jnp
from jax import lax
from jax.experimental import pallas as pl
from jax.experimental.pallas import tpu as pltpu
from jax.sharding import PartitionSpec as P

BLK = 128
NS_ITERS = 5
DAMPING = 0.1
DP = 4
TILE = BLK // DP
CORNER = TILE // 2
OCTAVES = 240
SCALE_ROWS = 16


SMALL = pltpu.CompilerParams(vmem_limit_bytes=4 * 1024 * 1024)
ANY = pl.BlockSpec(memory_space=pl.ANY)
VMEM = pl.BlockSpec(memory_space=pltpu.VMEM)
SMEM = pl.BlockSpec(memory_space=pltpu.SMEM)


def run(copies, sems):
    made = [pltpu.make_async_copy(source, target, sems.at[i]) for i, (source, target) in enumerate(copies)]
    for copy in made:
        copy.start()
    for copy in made:
        copy.wait()


def lane_tile(shape):
    return lax.broadcasted_iota(jnp.int32, shape, len(shape) - 1) // TILE


def turned(value, tiles):
    if isinstance(tiles, int):
        shift = tiles * TILE % BLK
        return pltpu.roll(value, shift, value.ndim - 1) if shift else value
    return pltpu.roll(value, lax.rem(tiles * TILE + 2 * BLK, BLK), value.ndim - 1)


def pack_state_kernel(a_ref, g_ref, out_ref, strip, corner, sems):
    part = lax.axis_index("dp")
    odd = lax.rem(part, 2)
    rows = pl.ds(pl.multiple_of(part * TILE, TILE), TILE)
    half = pl.ds(pl.multiple_of(odd * TILE + lax.div(part, 2) * CORNER, CORNER), CORNER)
    copies = []
    for which, ref in enumerate((a_ref, g_ref)):
        copies.append((ref.at[:, rows, :], strip.at[which]))
        copies.append((ref.at[:, half, :], corner.at[which]))
    run(copies, sems)

    sections = out_ref.shape[0]
    a, g = (strip[which].astype(jnp.float32).reshape(-1, BLK) for which in range(2))
    pairs = jnp.where(lane_tile(a.shape) < 2, turned(a, -part), turned(g, 2 - part))
    out_ref[:, :2 * TILE] = pairs.astype(out_ref.dtype).reshape(sections, 2 * TILE, BLK)

    a, g = (corner[which].astype(jnp.float32).reshape(sections, 2, CORNER, BLK) for which in range(2))
    tile = lane_tile((sections * CORNER, BLK))
    last = jnp.zeros(tile.shape, jnp.float32)
    for place, source in enumerate((a[:, 0], g[:, 0], a[:, 1], g[:, 1])):
        last = jnp.where(tile == place, turned(source.reshape(tile.shape), place - 2 - odd), last)
    out_ref[:, 2 * TILE:] = last.astype(out_ref.dtype).reshape(sections, CORNER, BLK)


def pack_state(state_a, state_g):
    slots = state_a.shape[0]
    state_a = pltpu.with_memory_space_constraint(state_a, pltpu.HBM)
    state_g = pltpu.with_memory_space_constraint(state_g, pltpu.HBM)
    return pl.pallas_call(
        pack_state_kernel,
        out_shape=pltpu.VMEM((slots // 2, 2 * TILE + CORNER, BLK), state_a.dtype),
        in_specs=[ANY, ANY],
        out_specs=VMEM,
        scratch_shapes=[
            pltpu.VMEM((2, slots, TILE, BLK), state_a.dtype),
            pltpu.VMEM((2, slots, CORNER, BLK), state_a.dtype),
            pltpu.SemaphoreType.DMA((4,)),
        ],
        compiler_params=pltpu.CompilerParams(vmem_limit_bytes=6 * 1024 * 1024),
        name="pack_state",
    )(state_a, state_g)


def pack_tokens_kernel(assign_ref, arrived_ref, embedded_ref, returned_ref, loss_ref, *refs):
    send_refs, (slot_ref, holder_ref, sems, holder_sem) = refs[:DP], refs[DP:]
    holders = pltpu.make_async_copy(assign_ref, holder_ref, holder_sem)
    holders.start()
    width = send_refs[0].shape[2]
    section, part = lax.axis_index("section"), lax.axis_index("dp")
    last_section = lax.axis_size("section") - 1

    for first in (True, False):
        for last in (True, False):
            if first and last:
                continue

            @pl.when(((section == 0) == first) & ((section == last_section) == last))
            def _():
                copies = []
                for which, source in enumerate((embedded_ref if first else arrived_ref, loss_ref if last else returned_ref)):
                    for turn in range(DP):
                        start = pl.multiple_of(lax.rem(part + turn, DP) * width, width)
                        copies.append((source.at[:, pl.ds(start, width)], send_refs[turn].at[which]))
                run(copies, sems)

    holders.wait()
    for j in range(holder_ref.shape[0]):
        rank = jnp.int32(0)
        for earlier in range(j):
            rank = rank + (holder_ref[earlier] == holder_ref[j]).astype(jnp.int32)
        slot_ref[j] = holder_ref[j] * 2 + rank


def pack_tokens(assign, arrived, embedded, returned, loss_grad):
    tokens, features = arrived.shape
    shape = jax.ShapeDtypeStruct((2, tokens, features // DP), arrived.dtype)
    assign = pltpu.with_memory_space_constraint(assign, pltpu.HBM)
    return pl.pallas_call(
        pack_tokens_kernel,
        out_shape=(shape,) * DP + (pltpu.SMEM(assign.shape, jnp.int32),),
        in_specs=[ANY] * 5,
        out_specs=(ANY,) * DP + (SMEM,),
        scratch_shapes=[
            pltpu.SMEM(assign.shape, jnp.int32),
            pltpu.SemaphoreType.DMA((2 * DP,)),
            pltpu.SemaphoreType.DMA,
        ],
        compiler_params=SMALL,
        cost_estimate=pl.CostEstimate(flops=15 * 10**9, bytes_accessed=2**20, transcendentals=0),
        name="pack_tokens",
    )(assign, arrived, embedded, returned, loss_grad)


def select_kernel(slot_ref, got_ref, out_ref):
    blocks = slot_ref.shape[0] // DP
    low = lane_tile((CORNER, BLK)) < 2
    for part in range(DP):
        corners = []
        for j in range(blocks):
            slot = slot_ref[part * blocks + j]
            holder, rank = lax.div(slot, 2), lax.rem(slot, 2)
            mine = pl.ds(pl.multiple_of(rank * TILE, TILE), TILE)
            out_ref[part, j * TILE:(j + 1) * TILE] = got_ref[holder, mine, :]
            corner = got_ref[holder, 2 * TILE:, :].astype(jnp.float32)
            corners.append(turned(corner, 2 * lax.rem(rank + j, 2)))
        for j in range(0, blocks, 2):
            both = jnp.where(low, corners[j], corners[min(j + 1, blocks - 1)])
            start = blocks * TILE + j // 2 * CORNER
            out_ref[part, start:start + CORNER] = both.astype(out_ref.dtype)


def select(slot, got):
    blocks = slot.shape[0] // DP
    return pl.pallas_call(
        select_kernel,
        out_shape=jax.ShapeDtypeStruct((DP, blocks * TILE + (blocks + 1) // 2 * CORNER, BLK), got.dtype),
        in_specs=[SMEM, VMEM],
        out_specs=VMEM,
        compiler_params=SMALL,
        name="select",
    )(slot, got)


def symmetric(held_ref, blocks, j, which):
    tile = lane_tile((TILE, BLK))
    start = blocks * TILE + j // 2 * CORNER
    corners = [held_ref[part, start:start + CORNER].astype(jnp.float32) for part in range(DP)]
    rows = []
    for part in range(DP):
        strip = turned(held_ref[part, j * TILE:(j + 1) * TILE].astype(jnp.float32), part - 2 * which)
        row = jnp.where(tile == part, 0.5 * strip, jnp.where(tile == (part + 1) % DP, strip, 0.0))
        if part < 2:
            corner = jnp.concatenate([corners[part], corners[part + 2]], axis=0)
            row = jnp.where(tile == part + 2, turned(corner, 2 + part - 2 * (j % 2) - which), row)
        rows.append(row)
    upper = jnp.concatenate(rows, axis=0)
    return upper + upper.T


def halves(value):
    high = value.astype(jnp.bfloat16)
    low = (value - high.astype(jnp.float32)).astype(jnp.bfloat16)
    return high, low


def product(left, right):
    lhs = jnp.concatenate([left[0], left[0], left[1]], axis=1)
    rhs = jnp.concatenate([right[0], right[1], right[0]], axis=0)
    return jnp.dot(lhs, rhs, preferred_element_type=jnp.float32)


def gram_kernel(*refs):
    chunk_refs, out_ref = refs[:-1], refs[-1]
    for j in range(out_ref.shape[0]):
        columns = slice(j * BLK, (j + 1) * BLK)
        inputs = jnp.concatenate([ref[0, :, columns] for ref in chunk_refs], axis=0)
        grads = jnp.concatenate([ref[1, :, columns] for ref in chunk_refs], axis=0)
        both = jnp.concatenate([inputs, grads], axis=1)
        out_ref[j] = lax.dot_general(both, both, (((0,), (0,)), ((), ())), preferred_element_type=jnp.float32)


def gram(chunks):
    return pl.pallas_call(
        gram_kernel,
        out_shape=jax.ShapeDtypeStruct((chunks[0].shape[2] // BLK, 2 * BLK, 2 * BLK), jnp.float32),
        in_specs=[VMEM] * DP,
        out_specs=VMEM,
        compiler_params=pltpu.CompilerParams(vmem_limit_bytes=8 * 1024 * 1024),
        cost_estimate=pl.CostEstimate(flops=10**9, bytes_accessed=2**20, transcendentals=0),
        name="gram",
    )(*chunks)


def coded(value):
    bound = jnp.max(jnp.abs(value), axis=0, keepdims=True)
    bound = jnp.maximum(bound * (1 + 2.0**-7), 1e-35).astype(jnp.bfloat16)
    place = jnp.abs(value) * (OCTAVES / bound.astype(jnp.float32))
    octave = jnp.floor(place)
    code = jnp.exp2(octave - OCTAVES // 2) * (1 + (place - octave))
    code = jnp.where(value < 0, -code, code).astype(jnp.bfloat16)
    return code, jnp.broadcast_to(bound, (SCALE_ROWS, BLK))


def decoded(code, bound):
    code = code.astype(jnp.float32)
    size = jnp.abs(code)
    octave = jnp.floor(jnp.log2(size))
    place = octave + (OCTAVES // 2 - 1) + size * jnp.exp2(-octave)
    value = place * (bound.astype(jnp.float32) / OCTAVES)
    return jnp.where(code < 0, -value, value)


def decode_kernel(got_ref, out_ref, values, sems):
    blocks = got_ref.shape[1]
    copies = []
    for part in range(DP):
        for j in range(blocks):
            at = part * blocks + j
            values[at] = decoded(got_ref[part, j, :BLK], got_ref[part, j, BLK:BLK + 1])
            copies.append(pltpu.make_async_copy(values.at[at], out_ref.at[at], sems.at[at]))
            copies[-1].start()
    for copy in copies:
        copy.wait()


def decode(got):
    blocks = DP * got.shape[1]
    return pl.pallas_call(
        decode_kernel,
        out_shape=pltpu.HBM((blocks, BLK, BLK), jnp.float32),
        in_specs=[VMEM],
        out_specs=ANY,
        scratch_shapes=[pltpu.VMEM((blocks, BLK, BLK), jnp.float32), pltpu.SemaphoreType.DMA((blocks,))],
        compiler_params=SMALL,
        name="decode",
    )(got)


def precondition_kernel(tokens_total, sums_ref, held_ref, out_ref):
    count = out_ref.shape[1]
    row = lax.broadcasted_iota(jnp.int32, (BLK, BLK), 0)
    column = lax.broadcasted_iota(jnp.int32, (BLK, BLK), 1)
    identity = (row == column).astype(jnp.float32)
    blocks = [(j, which) for j in range(count) for which in range(2)]
    bound, rest, inverse = {}, {}, {}
    for j, which in blocks:
        held = symmetric(held_ref, count, j, which)
        batch = sums_ref[j, BLK:, BLK:] if which else sums_ref[j, :BLK, :BLK] / tokens_total
        matrix = 0.5 * held + 0.5 * batch + DAMPING * identity
        bound[j, which] = jnp.max(jnp.sum(jnp.abs(matrix), axis=0, keepdims=True), axis=1, keepdims=True)
        rest[j, which] = identity - matrix / bound[j, which]
    for block in blocks:
        inverse[block] = identity + rest[block]
        parts = halves(rest[block])
        rest[block] = product(parts, parts)
    for step in range(1, NS_ITERS):
        for block in blocks:
            left, right = halves(rest[block]), halves(inverse[block])
            if step < NS_ITERS - 1:
                both = product(left, [jnp.concatenate([l, r], axis=1) for l, r in zip(left, right)])
                rest[block] = both[:, :BLK]
                inverse[block] = inverse[block] + both[:, BLK:]
            else:
                inverse[block] = inverse[block] + product(left, right)
    half_done = [
        product(halves(inverse[j, 0]), halves(sums_ref[j, :BLK, BLK:] / bound[j, 0])) for j in range(count)
    ]
    for j in range(count):
        code, scale = coded(product(halves(half_done[j]), halves(inverse[j, 1])) / bound[j, 1])
        for part in range(DP):
            out_ref[part, j, :BLK] = code
            out_ref[part, j, BLK:] = scale


def precondition(sums, held, tokens_total):
    return pl.pallas_call(
        functools.partial(precondition_kernel, tokens_total),
        out_shape=jax.ShapeDtypeStruct((DP, sums.shape[0], BLK + SCALE_ROWS, BLK), jnp.bfloat16),
        in_specs=[VMEM, VMEM],
        out_specs=VMEM,
        compiler_params=pltpu.CompilerParams(vmem_limit_bytes=8 * 1024 * 1024),
        name="precondition",
    )(sums, held)


def spread(array, axis):
    return lax.all_to_all(array, axis, split_axis=0, concat_axis=0, tiled=True)


def hop(array, axis, by):
    size = lax.axis_size(axis)
    return lax.ppermute(array, axis, [(i, (i + by) % size) for i in range(size)])


def body(section_out, embedded, section_grad, loss_grad, assign, state_a, state_g):
    tokens = embedded.shape[0]
    arrived = hop(section_out[0], "section", 1)
    packed, section_grad = lax.optimization_barrier((pack_state(state_a[0], state_g[0]), section_grad))
    returned = hop(section_grad[0], "section", -1)
    got = spread(packed, "section")

    *sends, slot = pack_tokens(assign[0, :, 0], arrived, embedded, returned, loss_grad)
    chunks = [sends[0]] + [hop(sends[turn], "dp", turn) for turn in range(1, DP)]

    held = spread(select(slot, got), "dp")

    result = precondition(gram(chunks), held, tokens * DP)
    return decode(spread(result, "dp"))[None]


def solution(mesh):
    in_specs = (
        P("section", "dp", "tensor"),
        P("dp", "tensor"),
        P("section", "dp", "tensor"),
        P("dp", "tensor"),
        P("section", "tensor", None),
        P("section", "tensor", None, None),
        P("section", "tensor", None, None),
    )
    out_specs = P("section", "tensor", None, None)
    return jax.shard_map(body, mesh=mesh, in_specs=in_specs, out_specs=out_specs, check_vma=False)
```

```python
import functools

import jax
import jax.numpy as jnp
from jax import lax
from jax.experimental import pallas as pl
from jax.experimental.pallas import tpu as pltpu
from jax.sharding import PartitionSpec as P

BLK = 128
NS_ITERS = 5
DAMPING = 0.1
DP = 4
TILE = BLK // DP
CORNER = TILE // 2
OCTAVES = 240
SCALE_ROWS = 16


SMALL = pltpu.CompilerParams(vmem_limit_bytes=4 * 1024 * 1024)
ANY = pl.BlockSpec(memory_space=pl.ANY)
VMEM = pl.BlockSpec(memory_space=pltpu.VMEM)
SMEM = pl.BlockSpec(memory_space=pltpu.SMEM)


def run(copies, sems):
    made = [pltpu.make_async_copy(source, target, sems.at[i]) for i, (source, target) in enumerate(copies)]
    for copy in made:
        copy.start()
    for copy in made:
        copy.wait()


def lane_tile(shape):
    return lax.broadcasted_iota(jnp.int32, shape, len(shape) - 1) // TILE


def turned(value, tiles):
    if isinstance(tiles, int):
        shift = tiles * TILE % BLK
        return pltpu.roll(value, shift, value.ndim - 1) if shift else value
    return pltpu.roll(value, lax.rem(tiles * TILE + 2 * BLK, BLK), value.ndim - 1)


def pack_state_kernel(a_ref, g_ref, out_ref, strip, corner, sems):
    part = lax.axis_index("dp")
    odd = lax.rem(part, 2)
    rows = pl.ds(pl.multiple_of(part * TILE, TILE), TILE)
    half = pl.ds(pl.multiple_of(odd * TILE + lax.div(part, 2) * CORNER, CORNER), CORNER)
    copies = []
    for which, ref in enumerate((a_ref, g_ref)):
        copies.append((ref.at[:, rows, :], strip.at[which]))
        copies.append((ref.at[:, half, :], corner.at[which]))
    run(copies, sems)

    sections = out_ref.shape[0]
    a, g = (strip[which].astype(jnp.float32).reshape(-1, BLK) for which in range(2))
    pairs = jnp.where(lane_tile(a.shape) < 2, turned(a, -part), turned(g, 2 - part))
    out_ref[:, :2 * TILE] = pairs.astype(out_ref.dtype).reshape(sections, 2 * TILE, BLK)

    a, g = (corner[which].astype(jnp.float32).reshape(sections, 2, CORNER, BLK) for which in range(2))
    tile = lane_tile((sections * CORNER, BLK))
    last = jnp.zeros(tile.shape, jnp.float32)
    for place, source in enumerate((a[:, 0], g[:, 0], a[:, 1], g[:, 1])):
        last = jnp.where(tile == place, turned(source.reshape(tile.shape), place - 2 - odd), last)
    out_ref[:, 2 * TILE:] = last.astype(out_ref.dtype).reshape(sections, CORNER, BLK)


def pack_state(state_a, state_g):
    slots = state_a.shape[0]
    state_a = pltpu.with_memory_space_constraint(state_a, pltpu.HBM)
    state_g = pltpu.with_memory_space_constraint(state_g, pltpu.HBM)
    return pl.pallas_call(
        pack_state_kernel,
        out_shape=pltpu.VMEM((slots // 2, 2 * TILE + CORNER, BLK), state_a.dtype),
        in_specs=[ANY, ANY],
        out_specs=VMEM,
        scratch_shapes=[
            pltpu.VMEM((2, slots, TILE, BLK), state_a.dtype),
            pltpu.VMEM((2, slots, CORNER, BLK), state_a.dtype),
            pltpu.SemaphoreType.DMA((4,)),
        ],
        compiler_params=pltpu.CompilerParams(vmem_limit_bytes=6 * 1024 * 1024),
        name="pack_state",
    )(state_a, state_g)


def pack_tokens_kernel(assign_ref, arrived_ref, embedded_ref, returned_ref, loss_ref, *refs):
    send_refs, (slot_ref, holder_ref, sems, holder_sem) = refs[:DP], refs[DP:]
    holders = pltpu.make_async_copy(assign_ref, holder_ref, holder_sem)
    holders.start()
    width = send_refs[0].shape[2]
    section, part = lax.axis_index("section"), lax.axis_index("dp")
    last_section = lax.axis_size("section") - 1

    for first in (True, False):
        for last in (True, False):
            if first and last:
                continue

            @pl.when(((section == 0) == first) & ((section == last_section) == last))
            def _():
                copies = []
                for which, source in enumerate((embedded_ref if first else arrived_ref, loss_ref if last else returned_ref)):
                    for turn in range(DP):
                        start = pl.multiple_of(lax.rem(part + turn, DP) * width, width)
                        copies.append((source.at[:, pl.ds(start, width)], send_refs[turn].at[which]))
                run(copies, sems)

    holders.wait()
    for j in range(holder_ref.shape[0]):
        rank = jnp.int32(0)
        for earlier in range(j):
            rank = rank + (holder_ref[earlier] == holder_ref[j]).astype(jnp.int32)
        slot_ref[j] = holder_ref[j] * 2 + rank


def pack_tokens(assign, arrived, embedded, returned, loss_grad):
    tokens, features = arrived.shape
    shape = jax.ShapeDtypeStruct((2, tokens, features // DP), arrived.dtype)
    assign = pltpu.with_memory_space_constraint(assign, pltpu.HBM)
    return pl.pallas_call(
        pack_tokens_kernel,
        out_shape=(shape,) * DP + (pltpu.SMEM(assign.shape, jnp.int32),),
        in_specs=[ANY] * 5,
        out_specs=(ANY,) * DP + (SMEM,),
        scratch_shapes=[
            pltpu.SMEM(assign.shape, jnp.int32),
            pltpu.SemaphoreType.DMA((2 * DP,)),
            pltpu.SemaphoreType.DMA,
        ],
        compiler_params=SMALL,
        cost_estimate=pl.CostEstimate(flops=15 * 10**9, bytes_accessed=2**20, transcendentals=0),
        name="pack_tokens",
    )(assign, arrived, embedded, returned, loss_grad)


def select_kernel(slot_ref, got_ref, out_ref):
    blocks = slot_ref.shape[0] // DP
    low = lane_tile((CORNER, BLK)) < 2
    for part in range(DP):
        corners = []
        for j in range(blocks):
            slot = slot_ref[part * blocks + j]
            holder, rank = lax.div(slot, 2), lax.rem(slot, 2)
            mine = pl.ds(pl.multiple_of(rank * TILE, TILE), TILE)
            out_ref[part, j * TILE:(j + 1) * TILE] = got_ref[holder, mine, :]
            corner = got_ref[holder, 2 * TILE:, :].astype(jnp.float32)
            corners.append(jnp.where(lax.rem(rank + j, 2) == 1, turned(corner, 2), corner))
        for j in range(0, blocks, 2):
            both = jnp.where(low, corners[j], corners[min(j + 1, blocks - 1)])
            start = blocks * TILE + j // 2 * CORNER
            out_ref[part, start:start + CORNER] = both.astype(out_ref.dtype)


def select(slot, got):
    blocks = slot.shape[0] // DP
    return pl.pallas_call(
        select_kernel,
        out_shape=jax.ShapeDtypeStruct((DP, blocks * TILE + (blocks + 1) // 2 * CORNER, BLK), got.dtype),
        in_specs=[SMEM, VMEM],
        out_specs=VMEM,
        compiler_params=SMALL,
        name="select",
    )(slot, got)


def symmetric(held_ref, blocks, j, which):
    tile = lane_tile((TILE, BLK))
    start = blocks * TILE + j // 2 * CORNER
    corners = [held_ref[part, start:start + CORNER].astype(jnp.float32) for part in range(DP)]
    rows = []
    for part in range(DP):
        strip = turned(held_ref[part, j * TILE:(j + 1) * TILE].astype(jnp.float32), part - 2 * which)
        row = jnp.where(tile == part, 0.5 * strip, jnp.where(tile == (part + 1) % DP, strip, 0.0))
        if part < 2:
            corner = jnp.concatenate([corners[part], corners[part + 2]], axis=0)
            row = jnp.where(tile == part + 2, turned(corner, 2 + part - 2 * (j % 2) - which), row)
        rows.append(row)
    upper = jnp.concatenate(rows, axis=0)
    return upper + upper.T


def halves(value):
    high = value.astype(jnp.bfloat16)
    low = (value - high.astype(jnp.float32)).astype(jnp.bfloat16)
    return high, low


def product(left, right):
    lhs = jnp.concatenate([left[0], left[0], left[1]], axis=1)
    rhs = jnp.concatenate([right[0], right[1], right[0]], axis=0)
    return jnp.dot(lhs, rhs, preferred_element_type=jnp.float32)


def gram_kernel(*refs):
    chunk_refs, out_ref = refs[:-1], refs[-1]
    for j in range(out_ref.shape[0]):
        columns = slice(j * BLK, (j + 1) * BLK)
        inputs = jnp.concatenate([ref[0, :, columns] for ref in chunk_refs], axis=0)
        grads = jnp.concatenate([ref[1, :, columns] for ref in chunk_refs], axis=0)
        both = jnp.concatenate([inputs, grads], axis=1)
        out_ref[j] = lax.dot_general(both, both, (((0,), (0,)), ((), ())), preferred_element_type=jnp.float32)


def gram(chunks):
    return pl.pallas_call(
        gram_kernel,
        out_shape=jax.ShapeDtypeStruct((chunks[0].shape[2] // BLK, 2 * BLK, 2 * BLK), jnp.float32),
        in_specs=[VMEM] * DP,
        out_specs=VMEM,
        compiler_params=pltpu.CompilerParams(vmem_limit_bytes=8 * 1024 * 1024),
        cost_estimate=pl.CostEstimate(flops=10**9, bytes_accessed=2**20, transcendentals=0),
        name="gram",
    )(*chunks)


def coded(value):
    bound = jnp.max(jnp.abs(value), axis=0, keepdims=True)
    bound = jnp.maximum(bound * (1 + 2.0**-7), 1e-35).astype(jnp.bfloat16)
    place = jnp.abs(value) * (OCTAVES / bound.astype(jnp.float32))
    octave = jnp.floor(place)
    code = jnp.exp2(octave - OCTAVES // 2) * (1 + (place - octave))
    code = jnp.where(value < 0, -code, code).astype(jnp.bfloat16)
    return code, bound


def decoded(code, bound):
    code = code.astype(jnp.float32)
    size = jnp.abs(code)
    octave = jnp.floor(jnp.log2(size))
    place = octave + (OCTAVES // 2 - 1) + size * jnp.exp2(-octave)
    value = place * (bound / OCTAVES)
    return jnp.where(code < 0, -value, value)


def decode_kernel(got_ref, out_ref, values, sems):
    blocks = got_ref.shape[1] // BLK
    copies = []
    for part in range(DP):
        scales = got_ref[part, blocks * BLK:].astype(jnp.float32)
        for j in range(blocks):
            at = part * blocks + j
            values[at] = decoded(got_ref[part, j * BLK:(j + 1) * BLK], scales[j:j + 1])
            copies.append(pltpu.make_async_copy(values.at[at], out_ref.at[at], sems.at[at]))
            copies[-1].start()
    for copy in copies:
        copy.wait()


def decode(got):
    blocks = DP * (got.shape[1] // BLK)
    return pl.pallas_call(
        decode_kernel,
        out_shape=pltpu.HBM((blocks, BLK, BLK), jnp.float32),
        in_specs=[VMEM],
        out_specs=ANY,
        scratch_shapes=[pltpu.VMEM((blocks, BLK, BLK), jnp.float32), pltpu.SemaphoreType.DMA((blocks,))],
        compiler_params=SMALL,
        name="decode",
    )(got)


def precondition_kernel(tokens_total, sums_ref, held_ref, out_ref):
    count = out_ref.shape[1] // BLK
    row = lax.broadcasted_iota(jnp.int32, (BLK, BLK), 0)
    column = lax.broadcasted_iota(jnp.int32, (BLK, BLK), 1)
    identity = (row == column).astype(jnp.float32)
    blocks = [(j, which) for j in range(count) for which in range(2)]
    scale, rest, inverse = {}, {}, {}
    for j, which in blocks:
        held = symmetric(held_ref, count, j, which)
        batch = sums_ref[j, BLK:, BLK:] if which else sums_ref[j, :BLK, :BLK] * (1 / tokens_total)
        matrix = 0.5 * held + 0.5 * batch + DAMPING * identity
        bound = jnp.max(jnp.sum(jnp.abs(matrix), axis=0, keepdims=True), axis=1, keepdims=True)
        scale[j, which] = 1 / bound
        rest[j, which] = identity - matrix * scale[j, which]
    for block in blocks:
        inverse[block] = identity + rest[block]
        parts = halves(rest[block])
        rest[block] = product(parts, parts)
    for step in range(1, NS_ITERS):
        for block in blocks:
            left, right = halves(rest[block]), halves(inverse[block])
            if step < NS_ITERS - 1:
                both = product(left, [jnp.concatenate([l, r], axis=1) for l, r in zip(left, right)])
                rest[block] = both[:, :BLK]
                inverse[block] = inverse[block] + both[:, BLK:]
            else:
                inverse[block] = inverse[block] + product(left, right)
    half_done = [
        product(halves(inverse[j, 0]), halves(sums_ref[j, :BLK, BLK:] * scale[j, 0])) for j in range(count)
    ]
    tops = jnp.zeros((SCALE_ROWS, BLK), jnp.float32)
    for j in range(count):
        code, top = coded(product(halves(half_done[j]), halves(inverse[j, 1])) * scale[j, 1])
        tops = jnp.where(row[:SCALE_ROWS] == j, top.astype(jnp.float32), tops)
        for part in range(DP):
            out_ref[part, j * BLK:(j + 1) * BLK] = code
    for part in range(DP):
        out_ref[part, count * BLK:] = tops.astype(out_ref.dtype)


def precondition(sums, held, tokens_total):
    return pl.pallas_call(
        functools.partial(precondition_kernel, tokens_total),
        out_shape=jax.ShapeDtypeStruct((DP, sums.shape[0] * BLK + SCALE_ROWS, BLK), jnp.bfloat16),
        in_specs=[VMEM, VMEM],
        out_specs=VMEM,
        compiler_params=pltpu.CompilerParams(vmem_limit_bytes=8 * 1024 * 1024),
        name="precondition",
    )(sums, held)


def spread(array, axis):
    return lax.all_to_all(array, axis, split_axis=0, concat_axis=0, tiled=True)


def hop(array, axis, by):
    size = lax.axis_size(axis)
    return lax.ppermute(array, axis, [(i, (i + by) % size) for i in range(size)])


def body(section_out, embedded, section_grad, loss_grad, assign, state_a, state_g):
    tokens = embedded.shape[0]
    arrived = hop(section_out[0], "section", 1)
    packed, section_grad = lax.optimization_barrier((pack_state(state_a[0], state_g[0]), section_grad))
    returned = hop(section_grad[0], "section", -1)
    got = spread(packed, "section")

    *sends, slot = pack_tokens(assign[0, :, 0], arrived, embedded, returned, loss_grad)
    chunks = [sends[0]] + [hop(sends[turn], "dp", turn) for turn in range(1, DP)]

    held = spread(select(slot, got), "dp")

    result = precondition(gram(chunks), held, tokens * DP)
    return decode(spread(result, "dp"))[None]


def solution(mesh):
    in_specs = (
        P("section", "dp", "tensor"),
        P("dp", "tensor"),
        P("section", "dp", "tensor"),
        P("dp", "tensor"),
        P("section", "tensor", None),
        P("section", "tensor", None, None),
        P("section", "tensor", None, None),
    )
    out_specs = P("section", "tensor", None, None)
    return jax.shard_map(body, mesh=mesh, in_specs=in_specs, out_specs=out_specs, check_vma=False)
```

```python
import functools

import jax
import jax.numpy as jnp
from jax import lax
from jax.experimental import pallas as pl
from jax.experimental.pallas import tpu as pltpu
from jax.sharding import PartitionSpec as P

BLK = 128
NS_ITERS = 5
DAMPING = 0.1
DP = 4
TILE = BLK // DP
CORNER = TILE // 2
OCTAVES = 240
SCALE_ROWS = 16


SMALL = pltpu.CompilerParams(vmem_limit_bytes=4 * 1024 * 1024)
ANY = pl.BlockSpec(memory_space=pl.ANY)
VMEM = pl.BlockSpec(memory_space=pltpu.VMEM)
SMEM = pl.BlockSpec(memory_space=pltpu.SMEM)


def run(copies, sems):
    made = [pltpu.make_async_copy(source, target, sems.at[i]) for i, (source, target) in enumerate(copies)]
    for copy in made:
        copy.start()
    for copy in made:
        copy.wait()


def lane_tile(shape):
    return lax.broadcasted_iota(jnp.int32, shape, len(shape) - 1) // TILE


def turned(value, tiles):
    if isinstance(tiles, int):
        shift = tiles * TILE % BLK
        return pltpu.roll(value, shift, value.ndim - 1) if shift else value
    return pltpu.roll(value, lax.rem(tiles * TILE + 2 * BLK, BLK), value.ndim - 1)


def pack_state_kernel(a_ref, g_ref, out_ref, strip, corner, sems):
    part = lax.axis_index("dp")
    odd = lax.rem(part, 2)
    rows = pl.ds(pl.multiple_of(part * TILE, TILE), TILE)
    half = pl.ds(pl.multiple_of(odd * TILE + lax.div(part, 2) * CORNER, CORNER), CORNER)
    copies = []
    for which, ref in enumerate((a_ref, g_ref)):
        copies.append((ref.at[:, rows, :], strip.at[which]))
        copies.append((ref.at[:, half, :], corner.at[which]))
    run(copies, sems)

    sections = out_ref.shape[0]
    a, g = (strip[which].astype(jnp.float32).reshape(-1, BLK) for which in range(2))
    pairs = jnp.where(lane_tile(a.shape) < 2, turned(a, -part), turned(g, 2 - part))
    out_ref[:, :2 * TILE] = pairs.astype(out_ref.dtype).reshape(sections, 2 * TILE, BLK)

    a, g = (corner[which].astype(jnp.float32).reshape(sections, 2, CORNER, BLK) for which in range(2))
    tile = lane_tile((sections * CORNER, BLK))
    last = jnp.zeros(tile.shape, jnp.float32)
    for place, source in enumerate((a[:, 0], g[:, 0], a[:, 1], g[:, 1])):
        last = jnp.where(tile == place, turned(source.reshape(tile.shape), place - 2 - odd), last)
    out_ref[:, 2 * TILE:] = last.astype(out_ref.dtype).reshape(sections, CORNER, BLK)


def pack_state(state_a, state_g):
    slots = state_a.shape[0]
    state_a = pltpu.with_memory_space_constraint(state_a, pltpu.HBM)
    state_g = pltpu.with_memory_space_constraint(state_g, pltpu.HBM)
    return pl.pallas_call(
        pack_state_kernel,
        out_shape=pltpu.VMEM((slots // 2, 2 * TILE + CORNER, BLK), state_a.dtype),
        in_specs=[ANY, ANY],
        out_specs=VMEM,
        scratch_shapes=[
            pltpu.VMEM((2, slots, TILE, BLK), state_a.dtype),
            pltpu.VMEM((2, slots, CORNER, BLK), state_a.dtype),
            pltpu.SemaphoreType.DMA((4,)),
        ],
        compiler_params=pltpu.CompilerParams(vmem_limit_bytes=6 * 1024 * 1024),
        name="pack_state",
    )(state_a, state_g)


def pack_tokens_kernel(assign_ref, arrived_ref, embedded_ref, returned_ref, loss_ref, *refs):
    send_refs, (slot_ref, holder_ref, sems, holder_sem) = refs[:DP], refs[DP:]
    holders = pltpu.make_async_copy(assign_ref, holder_ref, holder_sem)
    holders.start()
    width = send_refs[0].shape[2]
    section, part = lax.axis_index("section"), lax.axis_index("dp")
    last_section = lax.axis_size("section") - 1

    for first in (True, False):
        for last in (True, False):
            if first and last:
                continue

            @pl.when(((section == 0) == first) & ((section == last_section) == last))
            def _():
                copies = []
                for which, source in enumerate((embedded_ref if first else arrived_ref, loss_ref if last else returned_ref)):
                    for turn in range(DP):
                        start = pl.multiple_of(lax.rem(part + turn, DP) * width, width)
                        copies.append((source.at[:, pl.ds(start, width)], send_refs[turn].at[which]))
                run(copies, sems)

    holders.wait()
    for j in range(holder_ref.shape[0]):
        rank = jnp.int32(0)
        for earlier in range(j):
            rank = rank + (holder_ref[earlier] == holder_ref[j]).astype(jnp.int32)
        slot_ref[j] = holder_ref[j] * 2 + rank


def pack_tokens(assign, arrived, embedded, returned, loss_grad):
    tokens, features = arrived.shape
    shape = jax.ShapeDtypeStruct((2, tokens, features // DP), arrived.dtype)
    assign = pltpu.with_memory_space_constraint(assign, pltpu.HBM)
    return pl.pallas_call(
        pack_tokens_kernel,
        out_shape=(shape,) * DP + (pltpu.SMEM(assign.shape, jnp.int32),),
        in_specs=[ANY] * 5,
        out_specs=(ANY,) * DP + (SMEM,),
        scratch_shapes=[
            pltpu.SMEM(assign.shape, jnp.int32),
            pltpu.SemaphoreType.DMA((2 * DP,)),
            pltpu.SemaphoreType.DMA,
        ],
        compiler_params=SMALL,
        cost_estimate=pl.CostEstimate(flops=15 * 10**9, bytes_accessed=2**20, transcendentals=0),
        name="pack_tokens",
    )(assign, arrived, embedded, returned, loss_grad)


def select_kernel(slot_ref, got_ref, out_ref):
    blocks = slot_ref.shape[0] // DP
    low = lane_tile((CORNER, BLK)) < 2
    for part in range(DP):
        corners = []
        for j in range(blocks):
            slot = slot_ref[part * blocks + j]
            holder, rank = lax.div(slot, 2), lax.rem(slot, 2)
            mine = pl.ds(pl.multiple_of(rank * TILE, TILE), TILE)
            out_ref[part, j * TILE:(j + 1) * TILE] = got_ref[holder, mine, :]
            corner = got_ref[holder, 2 * TILE:, :].astype(jnp.float32)
            corners.append(jnp.where(lax.rem(rank + j, 2) == 1, turned(corner, 2), corner))
        for j in range(0, blocks, 2):
            both = jnp.where(low, corners[j], corners[min(j + 1, blocks - 1)])
            start = blocks * TILE + j // 2 * CORNER
            out_ref[part, start:start + CORNER] = both.astype(out_ref.dtype)


def select(slot, got):
    blocks = slot.shape[0] // DP
    return pl.pallas_call(
        select_kernel,
        out_shape=jax.ShapeDtypeStruct((DP, blocks * TILE + (blocks + 1) // 2 * CORNER, BLK), got.dtype),
        in_specs=[SMEM, VMEM],
        out_specs=VMEM,
        compiler_params=SMALL,
        name="select",
    )(slot, got)


def symmetric(held_ref, blocks, j, which):
    tile = lane_tile((TILE, BLK))
    start = blocks * TILE + j // 2 * CORNER
    corners = [held_ref[part, start:start + CORNER].astype(jnp.float32) for part in range(DP)]
    rows = []
    for part in range(DP):
        strip = turned(held_ref[part, j * TILE:(j + 1) * TILE].astype(jnp.float32), part - 2 * which)
        row = jnp.where(tile == part, 0.5 * strip, jnp.where(tile == (part + 1) % DP, strip, 0.0))
        if part < 2:
            corner = jnp.concatenate([corners[part], corners[part + 2]], axis=0)
            row = jnp.where(tile == part + 2, turned(corner, 2 + part - 2 * (j % 2) - which), row)
        rows.append(row)
    upper = jnp.concatenate(rows, axis=0)
    return upper + upper.T


def halves(value):
    high = value.astype(jnp.bfloat16)
    low = (value - high.astype(jnp.float32)).astype(jnp.bfloat16)
    return high, low


def product(left, right):
    lhs = jnp.concatenate([left[0], left[0], left[1]], axis=1)
    rhs = jnp.concatenate([right[0], right[1], right[0]], axis=0)
    return jnp.dot(lhs, rhs, preferred_element_type=jnp.float32)


def gram_kernel(*refs):
    chunk_refs, out_ref = refs[:-1], refs[-1]
    for j in range(out_ref.shape[0]):
        columns = slice(j * BLK, (j + 1) * BLK)
        inputs = jnp.concatenate([ref[0, :, columns] for ref in chunk_refs], axis=0)
        grads = jnp.concatenate([ref[1, :, columns] for ref in chunk_refs], axis=0)
        both = jnp.concatenate([inputs, grads], axis=1)
        out_ref[j] = lax.dot_general(both, both, (((0,), (0,)), ((), ())), preferred_element_type=jnp.float32)


def gram(chunks):
    return pl.pallas_call(
        gram_kernel,
        out_shape=jax.ShapeDtypeStruct((chunks[0].shape[2] // BLK, 2 * BLK, 2 * BLK), jnp.float32),
        in_specs=[VMEM] * DP,
        out_specs=VMEM,
        compiler_params=pltpu.CompilerParams(vmem_limit_bytes=8 * 1024 * 1024),
        cost_estimate=pl.CostEstimate(flops=10**9, bytes_accessed=2**20, transcendentals=0),
        name="gram",
    )(*chunks)


def coded(value):
    bound = jnp.max(jnp.abs(value), axis=0, keepdims=True)
    bound = jnp.maximum(bound * (1 + 2.0**-7), 1e-35).astype(jnp.bfloat16)
    place = jnp.abs(value) * (OCTAVES / bound.astype(jnp.float32))
    octave = jnp.floor(place)
    code = jnp.exp2(octave - OCTAVES // 2) * (1 + (place - octave))
    code = jnp.where(value < 0, -code, code).astype(jnp.bfloat16)
    return code, bound


def decoded(code, bound):
    code = code.astype(jnp.float32)
    size = jnp.abs(code)
    octave = jnp.floor(jnp.log2(size))
    place = octave + (OCTAVES // 2 - 1) + size * jnp.exp2(-octave)
    value = place * (bound / OCTAVES)
    return jnp.where(code < 0, -value, value)


def decode_kernel(got_ref, out_ref, values, sems):
    blocks = got_ref.shape[1] // BLK
    copies = []
    for part in range(DP):
        scales = got_ref[part, blocks * BLK:].astype(jnp.float32)
        for j in range(blocks):
            at = part * blocks + j
            values[at] = decoded(got_ref[part, j * BLK:(j + 1) * BLK], scales[j:j + 1])
            copies.append(pltpu.make_async_copy(values.at[at], out_ref.at[at], sems.at[at]))
            copies[-1].start()
    for copy in copies:
        copy.wait()


def decode(got):
    blocks = DP * (got.shape[1] // BLK)
    return pl.pallas_call(
        decode_kernel,
        out_shape=pltpu.HBM((blocks, BLK, BLK), jnp.float32),
        in_specs=[VMEM],
        out_specs=ANY,
        scratch_shapes=[pltpu.VMEM((blocks, BLK, BLK), jnp.float32), pltpu.SemaphoreType.DMA((blocks,))],
        compiler_params=SMALL,
        name="decode",
    )(got)


def precondition_kernel(tokens_total, sums_ref, held_ref, out_ref):
    count = out_ref.shape[1] // BLK
    row = lax.broadcasted_iota(jnp.int32, (BLK, BLK), 0)
    column = lax.broadcasted_iota(jnp.int32, (BLK, BLK), 1)
    identity = (row == column).astype(jnp.float32)
    blocks = [(j, which) for j in range(count) for which in range(2)]
    scale, rest, inverse = {}, {}, {}
    for j, which in blocks:
        held = symmetric(held_ref, count, j, which)
        batch = sums_ref[j, BLK:, BLK:] if which else sums_ref[j, :BLK, :BLK] * (1 / tokens_total)
        matrix = 0.5 * held + 0.5 * batch + DAMPING * identity
        bound = jnp.max(jnp.sum(jnp.abs(matrix), axis=0, keepdims=True), axis=1, keepdims=True)
        scale[j, which] = 1 / bound
        rest[j, which] = identity - matrix * scale[j, which]
    for block in blocks:
        inverse[block] = identity + rest[block]
        parts = halves(rest[block])
        rest[block] = product(parts, parts)
    for step in range(1, NS_ITERS):
        for block in blocks:
            left, right = halves(rest[block]), halves(inverse[block])
            if step < NS_ITERS - 1:
                both = product(left, [jnp.concatenate([l, r], axis=1) for l, r in zip(left, right)])
                rest[block] = both[:, :BLK]
                inverse[block] = inverse[block] + both[:, BLK:]
            else:
                inverse[block] = inverse[block] + product(left, right)
    half_done = [
        product(halves(inverse[j, 0]), halves(sums_ref[j, :BLK, BLK:] * scale[j, 0])) for j in range(count)
    ]
    tops = jnp.zeros((SCALE_ROWS, BLK), jnp.float32)
    for j in range(count):
        code, top = coded(product(halves(half_done[j]), halves(inverse[j, 1])) * scale[j, 1])
        tops = jnp.where(row[:SCALE_ROWS] == j, top.astype(jnp.float32), tops)
        for part in range(DP):
            out_ref[part, j * BLK:(j + 1) * BLK] = code
    for part in range(DP):
        out_ref[part, count * BLK:] = tops.astype(out_ref.dtype)


def precondition(sums, held, tokens_total):
    return pl.pallas_call(
        functools.partial(precondition_kernel, tokens_total),
        out_shape=jax.ShapeDtypeStruct((DP, sums.shape[0] * BLK + SCALE_ROWS, BLK), jnp.bfloat16),
        in_specs=[VMEM, VMEM],
        out_specs=VMEM,
        compiler_params=pltpu.CompilerParams(vmem_limit_bytes=8 * 1024 * 1024),
        name="precondition",
    )(sums, held)


def spread(array, axis):
    return lax.all_to_all(array, axis, split_axis=0, concat_axis=0, tiled=True)


def hop(array, axis, by):
    size = lax.axis_size(axis)
    return lax.ppermute(array, axis, [(i, (i + by) % size) for i in range(size)])


def body(section_out, embedded, section_grad, loss_grad, assign, state_a, state_g):
    tokens = embedded.shape[0]
    arrived = hop(section_out[0], "section", 1)
    packed, section_grad = lax.optimization_barrier((pack_state(state_a[0], state_g[0]), section_grad))
    returned = hop(section_grad[0], "section", -1)
    got = spread(packed, "section")

    *sends, slot = pack_tokens(assign[0, :, 0], arrived, embedded, returned, loss_grad)
    chunks = [sends[0]] + [hop(sends[turn], "dp", turn) for turn in (2, 3, 1)]

    held = spread(select(slot, got), "dp")

    result = precondition(gram(chunks), held, tokens * DP)
    return decode(spread(result, "dp"))[None]


def solution(mesh):
    in_specs = (
        P("section", "dp", "tensor"),
        P("dp", "tensor"),
        P("section", "dp", "tensor"),
        P("dp", "tensor"),
        P("section", "tensor", None),
        P("section", "tensor", None, None),
        P("section", "tensor", None, None),
    )
    out_specs = P("section", "tensor", None, None)
    return jax.shard_map(body, mesh=mesh, in_specs=in_specs, out_specs=out_specs, check_vma=False)
```

```python
import functools

import jax
import jax.numpy as jnp
from jax import lax
from jax.experimental import pallas as pl
from jax.experimental.pallas import tpu as pltpu
from jax.sharding import PartitionSpec as P

BLK = 128
NS_ITERS = 5
DAMPING = 0.1
DP = 4
TILE = BLK // DP
CORNER = TILE // 2
OCTAVES = 240
SCALE_ROWS = 16


SMALL = pltpu.CompilerParams(vmem_limit_bytes=4 * 1024 * 1024)
ANY = pl.BlockSpec(memory_space=pl.ANY)
VMEM = pl.BlockSpec(memory_space=pltpu.VMEM)
SMEM = pl.BlockSpec(memory_space=pltpu.SMEM)


def run(copies, sems):
    made = [pltpu.make_async_copy(source, target, sems.at[i]) for i, (source, target) in enumerate(copies)]
    for copy in made:
        copy.start()
    for copy in made:
        copy.wait()


def lane_tile(shape):
    return lax.broadcasted_iota(jnp.int32, shape, len(shape) - 1) // TILE


def turned(value, tiles):
    if isinstance(tiles, int):
        shift = tiles * TILE % BLK
        return pltpu.roll(value, shift, value.ndim - 1) if shift else value
    return pltpu.roll(value, lax.rem(tiles * TILE + 2 * BLK, BLK), value.ndim - 1)


def pack_state_kernel(a_ref, g_ref, out_ref, strip, corner, sems):
    part = lax.axis_index("dp")
    odd = lax.rem(part, 2)
    rows = pl.ds(pl.multiple_of(part * TILE, TILE), TILE)
    half = pl.ds(pl.multiple_of(odd * TILE + lax.div(part, 2) * CORNER, CORNER), CORNER)
    copies = []
    for which, ref in enumerate((a_ref, g_ref)):
        copies.append((ref.at[:, rows, :], strip.at[which]))
        copies.append((ref.at[:, half, :], corner.at[which]))
    run(copies, sems)

    sections = out_ref.shape[0]
    a, g = (strip[which].astype(jnp.float32).reshape(-1, BLK) for which in range(2))
    pairs = jnp.where(lane_tile(a.shape) < 2, turned(a, -part), turned(g, 2 - part))
    out_ref[:, :2 * TILE] = pairs.astype(out_ref.dtype).reshape(sections, 2 * TILE, BLK)

    a, g = (corner[which].astype(jnp.float32).reshape(sections, 2, CORNER, BLK) for which in range(2))
    tile = lane_tile((sections * CORNER, BLK))
    last = jnp.zeros(tile.shape, jnp.float32)
    for place, source in enumerate((a[:, 0], g[:, 0], a[:, 1], g[:, 1])):
        last = jnp.where(tile == place, turned(source.reshape(tile.shape), place - 2 - odd), last)
    out_ref[:, 2 * TILE:] = last.astype(out_ref.dtype).reshape(sections, CORNER, BLK)


def pack_state(state_a, state_g):
    slots = state_a.shape[0]
    state_a = pltpu.with_memory_space_constraint(state_a, pltpu.HBM)
    state_g = pltpu.with_memory_space_constraint(state_g, pltpu.HBM)
    return pl.pallas_call(
        pack_state_kernel,
        out_shape=pltpu.VMEM((slots // 2, 2 * TILE + CORNER, BLK), state_a.dtype),
        in_specs=[ANY, ANY],
        out_specs=VMEM,
        scratch_shapes=[
            pltpu.VMEM((2, slots, TILE, BLK), state_a.dtype),
            pltpu.VMEM((2, slots, CORNER, BLK), state_a.dtype),
            pltpu.SemaphoreType.DMA((4,)),
        ],
        compiler_params=pltpu.CompilerParams(vmem_limit_bytes=6 * 1024 * 1024),
        name="pack_state",
    )(state_a, state_g)


def pack_tokens_kernel(assign_ref, arrived_ref, embedded_ref, returned_ref, loss_ref, *refs):
    send_refs, (slot_ref, holder_ref, sems, holder_sem) = refs[:DP], refs[DP:]
    holders = pltpu.make_async_copy(assign_ref, holder_ref, holder_sem)
    holders.start()
    width = send_refs[0].shape[2]
    section, part = lax.axis_index("section"), lax.axis_index("dp")
    last_section = lax.axis_size("section") - 1

    for first in (True, False):
        for last in (True, False):
            if first and last:
                continue

            @pl.when(((section == 0) == first) & ((section == last_section) == last))
            def _():
                copies = []
                for which, source in enumerate((embedded_ref if first else arrived_ref, loss_ref if last else returned_ref)):
                    for turn in range(DP):
                        start = pl.multiple_of(lax.rem(part + turn, DP) * width, width)
                        copies.append((source.at[:, pl.ds(start, width)], send_refs[turn].at[which]))
                run(copies, sems)

    holders.wait()
    for j in range(holder_ref.shape[0]):
        rank = jnp.int32(0)
        for earlier in range(j):
            rank = rank + (holder_ref[earlier] == holder_ref[j]).astype(jnp.int32)
        slot_ref[j] = holder_ref[j] * 2 + rank


def pack_tokens(assign, arrived, embedded, returned, loss_grad):
    tokens, features = arrived.shape
    shape = jax.ShapeDtypeStruct((2, tokens, features // DP), arrived.dtype)
    assign = pltpu.with_memory_space_constraint(assign, pltpu.HBM)
    return pl.pallas_call(
        pack_tokens_kernel,
        out_shape=(shape,) * DP + (pltpu.SMEM(assign.shape, jnp.int32),),
        in_specs=[ANY] * 5,
        out_specs=(ANY,) * DP + (SMEM,),
        scratch_shapes=[
            pltpu.SMEM(assign.shape, jnp.int32),
            pltpu.SemaphoreType.DMA((2 * DP,)),
            pltpu.SemaphoreType.DMA,
        ],
        compiler_params=SMALL,
        cost_estimate=pl.CostEstimate(flops=15 * 10**9, bytes_accessed=2**20, transcendentals=0),
        name="pack_tokens",
    )(assign, arrived, embedded, returned, loss_grad)


def select_kernel(slot_ref, got_ref, out_ref):
    blocks = slot_ref.shape[0] // DP
    low = lane_tile((CORNER, BLK)) < 2
    for part in range(DP):
        corners = []
        for j in range(blocks):
            slot = slot_ref[part * blocks + j]
            holder, rank = lax.div(slot, 2), lax.rem(slot, 2)
            mine = pl.ds(pl.multiple_of(rank * TILE, TILE), TILE)
            out_ref[part, j * TILE:(j + 1) * TILE] = got_ref[holder, mine, :]
            corner = got_ref[holder, 2 * TILE:, :].astype(jnp.float32)
            corners.append(jnp.where(lax.rem(rank + j, 2) == 1, turned(corner, 2), corner))
        for j in range(0, blocks, 2):
            both = jnp.where(low, corners[j], corners[min(j + 1, blocks - 1)])
            start = blocks * TILE + j // 2 * CORNER
            out_ref[part, start:start + CORNER] = both.astype(out_ref.dtype)


def select(slot, got):
    blocks = slot.shape[0] // DP
    return pl.pallas_call(
        select_kernel,
        out_shape=jax.ShapeDtypeStruct((DP, blocks * TILE + (blocks + 1) // 2 * CORNER, BLK), got.dtype),
        in_specs=[SMEM, VMEM],
        out_specs=VMEM,
        compiler_params=SMALL,
        name="select",
    )(slot, got)


def symmetric(held_ref, blocks, j, which):
    tile = lane_tile((TILE, BLK))
    start = blocks * TILE + j // 2 * CORNER
    corners = [held_ref[part, start:start + CORNER].astype(jnp.float32) for part in range(DP)]
    rows = []
    for part in range(DP):
        strip = turned(held_ref[part, j * TILE:(j + 1) * TILE].astype(jnp.float32), part - 2 * which)
        row = jnp.where(tile == part, 0.5 * strip, jnp.where(tile == (part + 1) % DP, strip, 0.0))
        if part < 2:
            corner = jnp.concatenate([corners[part], corners[part + 2]], axis=0)
            row = jnp.where(tile == part + 2, turned(corner, 2 + part - 2 * (j % 2) - which), row)
        rows.append(row)
    upper = jnp.concatenate(rows, axis=0)
    return upper + upper.T


def halves(value):
    high = value.astype(jnp.bfloat16)
    low = (value - high.astype(jnp.float32)).astype(jnp.bfloat16)
    return high, low


def product(left, right):
    lhs = jnp.concatenate([left[0], left[0], left[1]], axis=1)
    rhs = jnp.concatenate([right[0], right[1], right[0]], axis=0)
    return jnp.dot(lhs, rhs, preferred_element_type=jnp.float32)


def gram_kernel(*refs):
    chunk_refs, out_ref = refs[:-1], refs[-1]
    for j in range(out_ref.shape[0]):
        columns = slice(j * BLK, (j + 1) * BLK)
        inputs = jnp.concatenate([ref[0, :, columns] for ref in chunk_refs], axis=0)
        grads = jnp.concatenate([ref[1, :, columns] for ref in chunk_refs], axis=0)
        both = jnp.concatenate([inputs, grads], axis=1)
        out_ref[j] = lax.dot_general(both, both, (((0,), (0,)), ((), ())), preferred_element_type=jnp.float32)


def gram(chunks):
    return pl.pallas_call(
        gram_kernel,
        out_shape=jax.ShapeDtypeStruct((chunks[0].shape[2] // BLK, 2 * BLK, 2 * BLK), jnp.float32),
        in_specs=[VMEM] * DP,
        out_specs=VMEM,
        compiler_params=pltpu.CompilerParams(vmem_limit_bytes=8 * 1024 * 1024),
        cost_estimate=pl.CostEstimate(flops=10**9, bytes_accessed=2**20, transcendentals=0),
        name="gram",
    )(*chunks)


def coded(value):
    bound = jnp.max(jnp.abs(value), axis=0, keepdims=True)
    bound = jnp.maximum(bound * (1 + 2.0**-7), 1e-35).astype(jnp.bfloat16)
    place = jnp.abs(value) * (OCTAVES / bound.astype(jnp.float32))
    octave = jnp.floor(place)
    code = jnp.exp2(octave - OCTAVES // 2) * (1 + (place - octave))
    code = jnp.where(value < 0, -code, code).astype(jnp.bfloat16)
    return code, bound


def decoded(code, bound):
    code = code.astype(jnp.float32)
    size = jnp.abs(code)
    octave = jnp.floor(jnp.log2(size))
    place = octave + (OCTAVES // 2 - 1) + size * jnp.exp2(-octave)
    value = place * (bound / OCTAVES)
    return jnp.where(code < 0, -value, value)


def decode_kernel(got_ref, out_ref, values, sems):
    blocks = got_ref.shape[1] // BLK
    copies = []
    for part in range(DP):
        scales = got_ref[part, blocks * BLK:].astype(jnp.float32)
        for j in range(blocks):
            at = part * blocks + j
            values[at] = decoded(got_ref[part, j * BLK:(j + 1) * BLK], scales[j:j + 1])
            copies.append(pltpu.make_async_copy(values.at[at], out_ref.at[at], sems.at[at]))
            copies[-1].start()
    for copy in copies:
        copy.wait()


def decode(got):
    blocks = DP * (got.shape[1] // BLK)
    return pl.pallas_call(
        decode_kernel,
        out_shape=pltpu.HBM((blocks, BLK, BLK), jnp.float32),
        in_specs=[VMEM],
        out_specs=ANY,
        scratch_shapes=[pltpu.VMEM((blocks, BLK, BLK), jnp.float32), pltpu.SemaphoreType.DMA((blocks,))],
        compiler_params=SMALL,
        name="decode",
    )(got)


def precondition_kernel(tokens_total, sums_ref, held_ref, out_ref):
    count = out_ref.shape[1] // BLK
    row = lax.broadcasted_iota(jnp.int32, (BLK, BLK), 0)
    column = lax.broadcasted_iota(jnp.int32, (BLK, BLK), 1)
    identity = (row == column).astype(jnp.float32)
    blocks = [(j, which) for j in range(count) for which in range(2)]
    scale, rest, inverse = {}, {}, {}
    for j, which in blocks:
        held = symmetric(held_ref, count, j, which)
        batch = sums_ref[j, BLK:, BLK:] if which else sums_ref[j, :BLK, :BLK] * (1 / tokens_total)
        matrix = 0.5 * held + 0.5 * batch + DAMPING * identity
        bound = jnp.max(jnp.sum(jnp.abs(matrix), axis=0, keepdims=True), axis=1, keepdims=True)
        scale[j, which] = 1 / bound
        rest[j, which] = identity - matrix * scale[j, which]
    for block in blocks:
        inverse[block] = identity + rest[block]
        parts = halves(rest[block])
        rest[block] = product(parts, parts)
    for step in range(1, NS_ITERS):
        for block in blocks:
            left, right = halves(rest[block]), halves(inverse[block])
            if step < NS_ITERS - 1:
                both = product(left, [jnp.concatenate([l, r], axis=1) for l, r in zip(left, right)])
                rest[block] = both[:, :BLK]
                inverse[block] = inverse[block] + both[:, BLK:]
            else:
                inverse[block] = inverse[block] + product(left, right)
    half_done = [
        product(halves(inverse[j, 0]), halves(sums_ref[j, :BLK, BLK:] * scale[j, 0])) for j in range(count)
    ]
    tops = jnp.zeros((SCALE_ROWS, BLK), jnp.float32)
    for j in range(count):
        code, top = coded(product(halves(half_done[j]), halves(inverse[j, 1])) * scale[j, 1])
        tops = jnp.where(row[:SCALE_ROWS] == j, top.astype(jnp.float32), tops)
        for part in range(DP):
            out_ref[part, j * BLK:(j + 1) * BLK] = code
    for part in range(DP):
        out_ref[part, count * BLK:] = tops.astype(out_ref.dtype)


def precondition(sums, held, tokens_total):
    return pl.pallas_call(
        functools.partial(precondition_kernel, tokens_total),
        out_shape=jax.ShapeDtypeStruct((DP, sums.shape[0] * BLK + SCALE_ROWS, BLK), jnp.bfloat16),
        in_specs=[VMEM, VMEM],
        out_specs=VMEM,
        compiler_params=pltpu.CompilerParams(vmem_limit_bytes=8 * 1024 * 1024),
        name="precondition",
    )(sums, held)


def spread(array, axis):
    return lax.all_to_all(array, axis, split_axis=0, concat_axis=0, tiled=True)


def hop(array, axis, by):
    size = lax.axis_size(axis)
    return lax.ppermute(array, axis, [(i, (i + by) % size) for i in range(size)])


def body(section_out, embedded, section_grad, loss_grad, assign, state_a, state_g):
    tokens = embedded.shape[0]
    arrived = hop(section_out[0], "section", 1)
    packed, section_grad = lax.optimization_barrier((pack_state(state_a[0], state_g[0]), section_grad))
    returned = hop(section_grad[0], "section", -1)
    got = spread(packed, "section")

    *sends, slot = pack_tokens(assign[0, :, 0], arrived, embedded, returned, loss_grad)
    chunks = [sends[0]] + [hop(sends[turn], "dp", turn) for turn in (3, 2, 1)]

    held = spread(select(slot, got), "dp")

    result = precondition(gram(chunks), held, tokens * DP)
    return decode(spread(result, "dp"))[None]


def solution(mesh):
    in_specs = (
        P("section", "dp", "tensor"),
        P("dp", "tensor"),
        P("section", "dp", "tensor"),
        P("dp", "tensor"),
        P("section", "tensor", None),
        P("section", "tensor", None, None),
        P("section", "tensor", None, None),
    )
    out_specs = P("section", "tensor", None, None)
    return jax.shard_map(body, mesh=mesh, in_specs=in_specs, out_specs=out_specs, check_vma=False)
```
